128 devices in a mesh: expert: 16 (over y, z), fsdp: 8 (over x, core).
Axes of the slice: x: 4, y: 4, z: 4, core: 2. Of those that a mesh axis runs over, the one named last changes fastest.
Arguments:
- layer_input: bfloat16 [16, 1024, 1024], P('expert', 'fsdp'), may hold values from -6 to 6
- segment_ids: int32 [16, 1024], P('expert'), may hold values from 0 to 3, as said below
- routes: int32 [16, 1024, 8], P('expert', 'fsdp'), may hold values from 0 to 31, all different within a row; in each aligned block of 128 rows (0 to 127, 128 to 255, ..., all dimensions but the last counted through in order) at most 64 rows name the same one
- attn_gain: bfloat16 [1024], P('fsdp'), may hold values from 0.099609375 to 1.8984375
- w_query: bfloat16 [1024, 1024], P('fsdp'), may hold values from -0.25 to 0.25
- w_key: bfloat16 [1024, 512], P('fsdp'), may hold values from -0.25 to 0.25
- w_value: bfloat16 [1024, 512], P('fsdp'), may hold values from -0.1875 to 0.1875
- w_output: bfloat16 [1024, 1024], P('fsdp'), may hold values from -1.5 to 1.5
- w_router: bfloat16 [1024, 32], P('fsdp'), may hold values from -0.09375 to 0.09375
- ffn_gain: bfloat16 [1024], P('fsdp'), may hold values from 0.099609375 to 1.8984375
- w_gate: bfloat16 [32, 1024, 512], P('expert', 'fsdp'), may hold values from -0.1875 to 0.1875
- w_up: bfloat16 [32, 1024, 512], P('expert', 'fsdp'), may hold values from -0.1875 to 0.1875
- w_down: bfloat16 [32, 512, 1024], P('expert', None, 'fsdp'), may hold values from -0.75 to 0.75
- cotangent: bfloat16 [16, 1024, 1024], P('expert', 'fsdp'), may hold values from -6 to 6
Outputs:
- layer_output: bfloat16 [16, 1024, 1024], P('expert', 'fsdp')
- grad_input: bfloat16 [16, 1024, 1024], P('expert', 'fsdp')
- grad_attn_gain: float32 [1024], P('fsdp')
- grad_query: float32 [1024, 1024], P('fsdp')
- grad_key: float32 [1024, 512], P('fsdp')
- grad_value: float32 [1024, 512], P('fsdp')
- grad_output_proj: float32 [1024, 1024], P('fsdp')
- grad_router: float32 [1024, 32], P('fsdp')
- grad_ffn_gain: float32 [1024], P('fsdp')
- grad_gate: float32 [32, 1024, 512], P('expert', 'fsdp')
- grad_up: float32 [32, 1024, 512], P('expert', 'fsdp')
- grad_down: float32 [32, 512, 1024], P('expert', None, 'fsdp')
The draws below stay inside these ranges and needn't reach their ends.
Inputs may be any that keep to these rules, and one draw needn't show every extreme that they name: `routes`: A token's 8 experts differ. In each aligned block of 128 tokens (one device's piece of one sequence) no expert is chosen by more than 64 tokens, and in some blocks one expert is chosen by exactly 64. `segment_ids`: never fall along a sequence and start at 0. On each index of expert, one of its 1 sequence has a document that begins in the first 128 tokens and ends in the last 128.
All inputs are finite; a program needn't handle non-finite values.
Results may differ from the reference program's by a relative error of at most 0.025.
Values may be sent and summed in bfloat16 or wider, within the bound.
No kernel may reach another device: no remote copies, remote signals or barrier semaphores. Data moves between devices by JAX's collectives and lax.ppermute only.
A program may use at most 192 MiB of HBM per device.

```python
import math
import jax
import jax.numpy as jnp
import numpy as np
from jax import lax

D = 1024
HEADS = 16
KV_HEADS = 8
HEAD_DIM = 64
FF = 512
TOP = 8
LENGTH = 1024
SEQS = 1
EXPERTS = 32
SEQUENCES = 16
LP = 128
MOST = 64
N_FSDP = 8


def draw_segment_ids(key, part):
    key = jax.random.fold_in(key, 7)
    first_key, last_key, middle_key, long_key = jax.random.split(key, 4)
    first_end = jax.random.randint(first_key, (SEQUENCES,), 1, LP)
    last_start = LENGTH - jax.random.randint(last_key, (SEQUENCES,), 1, LP)
    middle_cut = jax.random.randint(middle_key, (SEQUENCES,), first_end + 1, last_start)
    group_count = SEQUENCES // SEQS
    long_pick = jax.random.randint(long_key, (group_count,), 0, SEQS)
    seq_numbers = jnp.arange(SEQUENCES)
    is_long = seq_numbers % SEQS == long_pick[seq_numbers // SEQS]
    middle_cut = jnp.where(is_long, last_start, middle_cut)
    places = jnp.arange(LENGTH)[None, :]
    return (places >= first_end[:, None]).astype(jnp.int32) + (places >= middle_cut[:, None]).astype(jnp.int32) + (places >= last_start[:, None]).astype(jnp.int32)


def steps_of(own_key, extent, cuts, low, top_value):
    gain, own = 1.0, jax.random.fold_in(own_key, 6)
    for position, blocks in cuts:
        steps = jnp.exp(jax.random.uniform(jax.random.fold_in(own, position), (blocks,), jnp.float32, low / len(cuts), top_value / len(cuts)))
        gain = gain * jnp.repeat(steps, extent[position] // blocks).reshape([-1 if axis == position else 1 for axis in range(len(extent))])
    return gain


def deal_out(stream_key, own, number, rows, amount, top, most, lean):
    ranking = jax.random.permutation(stream_key, amount)
    heavy_load, usual = load_shares(amount, rows * top, most, lean, True), load_shares(amount, rows * top, most, lean, False)
    places = jnp.arange(amount)

    def named(tallies, offset_by):
        used = int((tallies > 0).sum())
        fixed = max(1, used // 4)
        passed = fixed + (places - fixed + offset_by * (used - fixed)) % max(1, amount - fixed)
        return jnp.zeros((amount,), jnp.int32).at[ranking[jnp.where(places < fixed, places, passed)]].set(jnp.asarray(tallies, jnp.int32))

    tallies = jnp.where(number % 4 == 0, named(heavy_load, number // 4), named(usual, number - number // 4 - 1))
    mixed = jax.random.permutation(jax.random.fold_in(own, 3), amount)
    donor, taker = mixed[0:amount // 2 * 2:2], mixed[1:amount // 2 * 2:2]
    room = jnp.minimum(tallies[donor] - 1, most - tallies[taker]) // 2
    room = jnp.where((donor == ranking[0]) | (taker == ranking[0]) | (tallies[taker] == 0), 0, jnp.maximum(room, 0))
    passed = jax.random.randint(jax.random.fold_in(own, 4), (amount // 2,), 0, 1 << 20) % (room + 1)
    tallies = tallies.at[donor].add(-passed).at[taker].add(passed)
    members = jnp.searchsorted(jnp.cumsum(tallies), jnp.arange(rows * top), side="right").astype(jnp.int32)
    grid = members.reshape(top, rows).T
    grid = grid[jax.random.permutation(jax.random.fold_in(own, 1), rows)]
    offset_by = jax.random.randint(jax.random.fold_in(own, 2), (rows, 1), 0, top)
    return jnp.take_along_axis(grid, (jnp.arange(top)[None, :] + offset_by) % top, axis=1)


def load_shares(amount, total, reach, lean, full):
    weights = [(1 << 20) // math.isqrt(grade ** lean) + 1 for grade in range(1, amount + 1)]
    largest = reach if full else min(reach, max(-(-total // amount), total * weights[0] // sum(weights)))
    least = 1 if total - largest >= amount - 1 else 0
    holding, spare = [largest] + [least] * (amount - 1), total - largest - least * (amount - 1)
    while spare > 0:
        candidates = [i for i in range(1, amount) if holding[i] < largest] or [i for i in range(1, amount) if holding[i] < reach]
        whole, left = sum([weights[i] for i in candidates]), spare
        for i in candidates:
            addition = min(reach - holding[i], max(1, left * weights[i] // whole), spare)
            holding[i] = holding[i] + addition
            spare = spare - addition
    return np.array(holding)


def noise(key, dims, width, bound, cuts=(), kind=jnp.bfloat16):
    array = width * jax.random.normal(key, dims, jnp.float32)
    if cuts:
        array = array * steps_of(key, dims, cuts, -0.22, 0.18)
    return jnp.clip(array, -bound, bound).astype(kind)


def setup_inputs(seed: int = 0) -> dict:
    splits = jax.random.split(jax.random.key(seed), 15)
    layer_input = noise(splits[0], (SEQUENCES, LENGTH, D), 1.0, 6.0, ((0, 16), (1, 8)))
    segment_ids = draw_segment_ids(jax.random.fold_in(splits[14], 71), 0)
    routes_keys = jax.random.split(jax.random.fold_in(splits[2], 1), SEQUENCES * LENGTH // LP)
    routes_turns = jax.random.permutation(jax.random.fold_in(splits[2], 3), SEQUENCES * LENGTH // LP)
    routes = jax.vmap(lambda own, number: deal_out(jax.random.fold_in(splits[2], 2), own, number, LP, EXPERTS, TOP, MOST, 2))(routes_keys, routes_turns).reshape((SEQUENCES, LENGTH, TOP))
    attn_gain = jnp.clip(1.0 + 0.18 * jax.random.normal(splits[3], (D,), jnp.float32), 0.099609375, 1.8984375).astype(jnp.bfloat16)
    w_query = noise(splits[4], (D, HEADS * HEAD_DIM), (D // 2) ** -0.5, 0.25, ((0, 8),))
    w_key = noise(splits[5], (D, KV_HEADS * HEAD_DIM), (D // 2) ** -0.5, 0.25, ((0, 8),))
    w_value = noise(splits[6], (D, KV_HEADS * HEAD_DIM), D ** -0.5, 0.1875, ((0, 8),))
    w_output = noise(splits[7], (HEADS * HEAD_DIM, D), (max(HEADS * HEAD_DIM // 64, 1)) ** -0.5, 1.5, ((0, 8),))
    w_router = noise(splits[8], (D, EXPERTS), (4 * D) ** -0.5, 0.09375, ((0, 8),))
    ffn_gain = jnp.clip(1.0 + 0.18 * jax.random.normal(splits[9], (D,), jnp.float32), 0.099609375, 1.8984375).astype(jnp.bfloat16)
    w_gate = noise(splits[10], (EXPERTS, D, FF), D ** -0.5, 0.1875, ((0, 16), (1, 8)))
    w_up = noise(splits[11], (EXPERTS, D, FF), D ** -0.5, 0.1875, ((0, 16), (1, 8)))
    w_down = noise(splits[12], (EXPERTS, FF, D), (FF // 8) ** -0.5, 0.75, ((0, 16), (2, 8)))
    cotangent = noise(splits[13], (SEQUENCES, LENGTH, D), 1.0, 6.0, ((0, 16), (1, 8)))
    return dict(layer_input=layer_input, segment_ids=segment_ids, routes=routes, attn_gain=attn_gain, w_query=w_query, w_key=w_key, w_value=w_value, w_output=w_output, w_router=w_router, ffn_gain=ffn_gain, w_gate=w_gate, w_up=w_up, w_down=w_down, cotangent=cotangent)


@jax.custom_vjp
def low(v):
    return lax.optimization_barrier(v.astype(jnp.bfloat16)).astype(jnp.float32)

@jax.custom_vjp
def low_back(v):
    return v

def low_keep(v):
    return (low(v), None)

def low_pass(kept, grad):
    return (grad,)

def back_keep(v):
    return (v, None)

def back_low(kept, grad):
    return (low(grad),)
low.defvjp(low_keep, low_pass)
low_back.defvjp(back_keep, back_low)
epsilon = 1e-06
rope_base = 10000.0
highest = lax.Precision.HIGHEST

def rms_scale(values, gain_vec):
    return values * lax.rsqrt(lax.optimization_barrier(jnp.mean(values * values, axis=-1, keepdims=True)) + epsilon) * gain_vec

def rope_tables(positions, head_width):
    half_width = head_width // 2
    exponent = jnp.arange(half_width).astype(jnp.float32) * (2.0 / head_width)
    inverse = rope_base ** (-exponent)
    angles = positions.astype(jnp.float32)[:, None] * inverse[None, :]
    return (jnp.cos(angles), jnp.sin(angles))

def rotate(vectors, cosine_tab, sine_tab):
    half_width = vectors.shape[-1] // 2
    first_half = vectors[..., :half_width]
    second_half = vectors[..., half_width:]
    cosine_b = cosine_tab[:, None, :]
    sine_b = sine_tab[:, None, :]
    return jnp.concatenate([first_half * cosine_b - second_half * sine_b, second_half * cosine_b + first_half * sine_b], axis=-1)

def pack_attention(items_in):
    query_rot, key_rot, value_low, segments = items_in
    length_all = query_rot.shape[0]
    groups = HEADS // KV_HEADS
    query_h = query_rot.reshape(length_all, KV_HEADS, groups, HEAD_DIM)
    scores = jnp.einsum('qhgd,khd->hgqk', query_h, key_rot, precision=highest) * HEAD_DIM ** (-0.5)
    scores = low_back(scores)
    places = jnp.arange(length_all)
    allowed = (segments[:, None] == segments[None, :]) & (places[None, :] <= places[:, None])
    scores = jnp.where(allowed, scores, -1e+30)
    probs_low = low(jax.nn.softmax(scores, axis=-1))
    mixed_heads = jnp.einsum('hgqk,khd->qhgd', probs_low, value_low, precision=highest)
    return low(low_back(mixed_heads.reshape(length_all, HEADS * HEAD_DIM)))

def forward(layer_input, attn_gain, w_query, w_key, w_value, w_output, w_router, ffn_gain, w_gate, w_up, w_down, segment_ids, routes):
    seq_total = layer_input.shape[0]
    normed = low(rms_scale(layer_input, attn_gain))
    cosine_tab, sine_tab = rope_tables(jnp.arange(LENGTH), HEAD_DIM)
    q_raw = low_back(jnp.dot(normed, w_query, precision=highest))
    k_raw = low_back(jnp.dot(normed, w_key, precision=highest))
    v_raw = low_back(jnp.dot(normed, w_value, precision=highest))
    query_rot = low(rotate(q_raw.reshape(seq_total, LENGTH, HEADS, HEAD_DIM), cosine_tab, sine_tab))
    key_rot = low(rotate(k_raw.reshape(seq_total, LENGTH, KV_HEADS, HEAD_DIM), cosine_tab, sine_tab))
    value_low = low(v_raw.reshape(seq_total, LENGTH, KV_HEADS, HEAD_DIM))
    attended = lax.map(jax.checkpoint(pack_attention), (query_rot, key_rot, value_low, segment_ids))
    branch = low_back(jnp.dot(attended, w_output, precision=highest))
    after_attn = layer_input + branch
    normed_two = low(rms_scale(after_attn, ffn_gain))
    logits = jnp.dot(normed_two, w_router, precision=highest)
    chosen = jnp.take_along_axis(logits, routes, axis=-1)
    gate_soft = jax.nn.softmax(chosen, axis=-1)
    tok_total = seq_total * LENGTH
    flat_rows = normed_two.reshape(tok_total, D)
    flat_routes = routes.reshape(tok_total, TOP)
    flat_gates = gate_soft.reshape(tok_total, TOP)
    padded_rows = jnp.concatenate([flat_rows, jnp.zeros((1, D), flat_rows.dtype)], axis=0)
    bound_rows = SEQUENCES * N_FSDP * MOST

    def expert_step(running, items_in):
        expert_id, gate_mat, up_mat, down_mat = items_in
        member = flat_routes == expert_id
        weight_col = lax.optimization_barrier(jnp.sum(jnp.where(member, flat_gates, 0.0), axis=-1))
        picked_rows = jnp.nonzero(jnp.any(member, axis=-1), size=bound_rows, fill_value=tok_total)[0]
        inputs_e = low_back(padded_rows[picked_rows])
        gate_val = low_back(jnp.dot(inputs_e, gate_mat, precision=highest))
        up_val = low_back(jnp.dot(inputs_e, up_mat, precision=highest))
        hidden = low(jax.nn.silu(gate_val) * up_val)
        result = low(low_back(jnp.dot(hidden, down_mat, precision=highest)))
        padded_weight = jnp.concatenate([weight_col, jnp.zeros((1,), weight_col.dtype)])
        running = running.at[picked_rows].add(padded_weight[picked_rows][:, None] * result)
        return (running, None)
    mixture, unused = lax.scan(jax.checkpoint(expert_step), jnp.zeros((tok_total + 1, D), jnp.float32), (jnp.arange(EXPERTS).astype(jnp.int32), w_gate, w_up, w_down))
    return after_attn + mixture[:tok_total].reshape(seq_total, LENGTH, D)

def reference(layer_input, segment_ids, routes, attn_gain, w_query, w_key, w_value, w_output, w_router, ffn_gain, w_gate, w_up, w_down, cotangent):
    arrays = tuple((array_in.astype(jnp.float32) for array_in in (layer_input, attn_gain, w_query, w_key, w_value, w_output, w_router, ffn_gain, w_gate, w_up, w_down)))

    def wrapped(layer_x, gain_one, query_mat, key_mat, value_mat, output_mat, router_mat, gain_two, gate_mats, up_mats, down_mats):
        return forward(layer_x, gain_one, query_mat, key_mat, value_mat, output_mat, router_mat, gain_two, gate_mats, up_mats, down_mats, segment_ids, routes)
    output, pull_back = jax.vjp(wrapped, *arrays)
    gradients = pull_back(cotangent.astype(jnp.float32))
    return (output.astype(jnp.bfloat16), gradients[0].astype(jnp.bfloat16), gradients[1], gradients[2], gradients[3], gradients[4], gradients[5], gradients[6], gradients[7], gradients[8], gradients[9], gradients[10])
```

```python
import jax
import jax.numpy as jnp
from jax import lax
from jax.sharding import PartitionSpec as P

HEAD_DIM = 64
EXPERTS = 32
SLOTS = 64
NF = 8
NE = 16
LP = 128
LENGTH = 1024
D = 1024
FF = 512

epsilon = 1e-06
rope_base = 10000.0
highest = lax.Precision.HIGHEST
bf16 = jnp.bfloat16
f32 = jnp.float32


def shift_x(v, k):
    return lax.ppermute(v, "fsdp", [(i, (i + 2 * k) % NF) for i in range(NF)])


def swap_core(v):
    return lax.ppermute(v, "fsdp", [(i, i ^ 1) for i in range(NF)])


def shift_z(v, k):
    return lax.ppermute(v, "expert", [(i, (i // 4) * 4 + (i + k) % 4) for i in range(NE)])


def shift_y(v, k):
    return lax.ppermute(v, "expert", [(i, (i + 4 * k) % NE) for i in range(NE)])


def put(buffer, piece, place):
    return lax.dynamic_update_index_in_dim(buffer, piece, place, 0)


def ring_gather(shift, v, place):
    got = [(v, place)] + [(shift(v, k), (place - k) % 4) for k in (1, 3, 2)]
    out = jnp.zeros((4,) + v.shape, v.dtype)
    for piece, where in got:
        out = put(out, piece, where)
    return out


def gather_fsdp(v):
    f = lax.axis_index("fsdp")
    x, c = f // 2, f % 2
    mine = ring_gather(shift_x, v, x)
    other = swap_core(mine)
    first = jnp.where(c == 0, mine, other)
    second = jnp.where(c == 0, other, mine)
    return jnp.stack([first, second], axis=1).reshape((NF,) + v.shape)


def gather_expert(v):
    e = lax.axis_index("expert")
    y, z = e // 4, e % 4
    n = v.shape[0] // 2
    a = ring_gather(shift_z, v[:n], z)
    b = ring_gather(shift_y, v[n:], y)
    a = ring_gather(shift_y, a, y)
    b = ring_gather(shift_z, b, z)
    return jnp.concatenate([a, jnp.swapaxes(b, 0, 1)], axis=2).reshape((NE,) + v.shape)


def ring_sum(shift, p, place):
    total = lax.dynamic_index_in_dim(p, place, 0, keepdims=False).astype(f32)
    for k in (1, 3, 2):
        piece = lax.dynamic_index_in_dim(p, (place + k) % 4, 0, keepdims=False)
        total = total + shift(piece, k).astype(f32)
    return total


def scatter_expert(p):
    e = lax.axis_index("expert")
    y, z = e // 4, e % 4
    n = p.shape[1] // 2
    p = p.reshape((4, 4) + p.shape[1:])
    a = p[:, :, :n]
    b = jnp.swapaxes(p[:, :, n:], 0, 1)
    a = ring_sum(shift_y, a, y).astype(bf16)
    b = ring_sum(shift_z, b, z).astype(bf16)
    a = ring_sum(shift_z, a, z)
    b = ring_sum(shift_y, b, y)
    return jnp.concatenate([a, b], axis=0)


def swap_fsdp(v):
    return lax.all_to_all(v, "fsdp", split_axis=0, concat_axis=0, tiled=True)


def rope_tables(positions):
    half_width = HEAD_DIM // 2
    exponent = jnp.arange(half_width).astype(f32) * (2.0 / HEAD_DIM)
    inverse = rope_base ** (-exponent)
    angles = positions.astype(f32)[:, None] * inverse[None, :]
    return (jnp.cos(angles), jnp.sin(angles))


def rotate(vectors, cosine_tab, sine_tab):
    a, b = vectors[..., : HEAD_DIM // 2], vectors[..., HEAD_DIM // 2 :]
    cos, sin = cosine_tab[:, None, :], sine_tab[:, None, :]
    return jnp.concatenate([a * cos - b * sin, b * cos + a * sin], axis=-1)


def masked_gates(logits, member):
    low = jnp.where(member, logits, -1e30)
    top = jnp.max(low, axis=-1, keepdims=True)
    expo = jnp.where(member, jnp.exp(low - top), 0.0)
    return expo / jnp.sum(expo, axis=-1, keepdims=True)


def norm_back(u, v, gain):
    r = lax.rsqrt(jnp.mean(v * v, axis=-1, keepdims=True) + epsilon)
    inner = jnp.mean(gain * u * v, axis=-1, keepdims=True)
    return r * gain * u - v * (r * r * r) * inner, jnp.sum(u * v * r, axis=0)


def local(
    layer_input,
    segment_ids,
    routes,
    attn_gain,
    w_query,
    w_key,
    w_value,
    w_output,
    w_router,
    ffn_gain,
    w_gate,
    w_up,
    w_down,
    cotangent,
):
    e = lax.axis_index("expert")
    x_own = layer_input[0]
    cot_own = cotangent[0]
    columns = jnp.concatenate(
        [
            w_query.reshape(LP, NF, 128),
            w_key.reshape(LP, NF, 64),
            w_value.reshape(LP, NF, 64),
        ],
        axis=-1,
    ).swapaxes(0, 1)
    extra = jnp.concatenate(
        [
            jnp.concatenate([attn_gain, ffn_gain])[None],
            w_router.reshape(16, 256),
            jnp.zeros((15, 256), bf16),
        ],
        axis=0,
    )
    payload = jnp.concatenate([columns, jnp.broadcast_to(extra[None], (NF, 32, 256))], axis=1)
    got = swap_fsdp(payload)
    x_all = gather_fsdp(x_own).reshape(LENGTH, D)
    w_qkv = got[:, :LP].reshape(D, 256)
    gain_one = got[:, LP, :128].reshape(D).astype(f32)
    gain_two = got[:, LP, 128:].reshape(D).astype(f32)
    router = got[:, LP + 1 : LP + 17].reshape(D, EXPERTS)
    w_out = lax.all_gather(w_output, "fsdp", axis=0, tiled=True)
    w_gu = lax.all_gather(jnp.concatenate([w_gate, w_up], axis=-1), "fsdp", axis=0)
    w_gu = w_gu.swapaxes(0, 1).reshape(2, D, 2 * FF)
    w_dn = lax.all_gather(w_down, "fsdp", axis=0)
    w_dn = w_dn.transpose(1, 2, 0, 3).reshape(2, FF, D)
    cot_all = gather_expert(cot_own)
    routes_all = lax.all_gather(routes[0], "expert", axis=0)

    own_ids = 2 * e + jnp.arange(2, dtype=jnp.int32)
    chosen_own = jnp.any(routes_all[:, :, :, None] == own_ids, axis=2)
    before = (jnp.arange(LP)[:, None] > jnp.arange(LP)[None, :]).astype(bf16)
    rank = jnp.einsum(
        "ts,bsj->jbt", before, chosen_own.astype(bf16), preferred_element_type=f32
    )
    member_t = chosen_own.transpose(2, 0, 1)
    pick = (
        (rank[:, :, None, :] == jnp.arange(SLOTS, dtype=f32)[:, None]) & member_t[:, :, None, :]
    ).astype(bf16)
    member_all = jnp.any(
        routes_all[:, :, :, None] == jnp.arange(EXPERTS, dtype=jnp.int32), axis=2
    )
    member_own = jnp.any(
        routes[0][:, :, None] == jnp.arange(EXPERTS, dtype=jnp.int32), axis=1
    )
    cot_slots = jnp.einsum("jbst,btd->jbsd", pick, cot_all, preferred_element_type=bf16).reshape(
        2, NE * SLOTS, D
    )

    x_full = x_all.astype(f32)
    r_one = lax.rsqrt(jnp.mean(x_full * x_full, axis=-1, keepdims=True) + epsilon)
    normed = (x_full * r_one * gain_one).astype(bf16)
    qkv = jnp.dot(normed, w_qkv, preferred_element_type=f32)
    cosine_tab, sine_tab = rope_tables(jnp.arange(LENGTH))
    rotated = rotate(qkv[:, :192].reshape(LENGTH, 3, HEAD_DIM), cosine_tab, sine_tab).astype(bf16)
    query, key = rotated[:, :2], rotated[:, 2]
    value = qkv[:, 192:].astype(bf16)
    seg = segment_ids[0]
    places = jnp.arange(LENGTH)
    allowed = (seg[:, None] == seg[None, :]) & (places[None, :] <= places[:, None])
    scale = HEAD_DIM**-0.5
    scores = jnp.einsum("qhd,kd->hqk", query, key, preferred_element_type=f32) * scale
    scores = jnp.where(allowed, scores, -1e30)
    row_top = jnp.max(scores, axis=-1, keepdims=True)
    expo = jnp.exp(scores - row_top)
    total = jnp.sum(expo, axis=-1, keepdims=True)
    probs = expo / total
    probs_low = probs.astype(bf16)
    attended = jnp.einsum("hqk,kd->qhd", probs_low, value, preferred_element_type=f32)
    attended = attended.reshape(LENGTH, 128).astype(bf16)
    attended_own = swap_fsdp(attended.reshape(NF, LP, 128)).swapaxes(0, 1).reshape(LP, D)
    after_attn = x_own.astype(f32) + jnp.dot(attended_own, w_out, preferred_element_type=f32)
    r_two = lax.rsqrt(jnp.mean(after_attn * after_attn, axis=-1, keepdims=True) + epsilon)
    normed_two = (after_attn * r_two * gain_two).astype(bf16)

    rows_all = gather_expert(normed_two)
    logits_all = jnp.einsum("btd,de->bte", rows_all, router, preferred_element_type=f32)
    gates_all = masked_gates(logits_all, member_all)
    gates_pair = lax.dynamic_slice_in_dim(gates_all, 2 * e, 2, axis=2).transpose(2, 0, 1)
    pick_f = pick.astype(f32)
    gate_slots = jnp.sum(pick_f * gates_pair[:, :, None, :], axis=-1).reshape(2, NE * SLOTS, 1)
    inputs = jnp.einsum("jbst,btd->jbsd", pick, rows_all, preferred_element_type=bf16).reshape(
        2, NE * SLOTS, D
    )
    both = jnp.einsum("jrd,jdf->jrf", inputs, w_gu, preferred_element_type=f32)
    gate_val, up_val = both[..., :FF], both[..., FF:]
    sig = jax.nn.sigmoid(gate_val)
    activated = gate_val * sig
    hidden = (activated * up_val).astype(bf16)
    result = jnp.einsum("jrf,jfd->jrd", hidden, w_dn, preferred_element_type=f32).astype(bf16)
    cot_f = cot_slots.astype(f32)
    result_f = result.astype(f32)
    dgate_slots = jnp.sum(result_f * cot_f, axis=-1).reshape(2, NE, SLOTS)
    weighted = (gate_slots * result_f).astype(bf16).reshape(2, NE, SLOTS, D)
    mix_part = jnp.einsum("jbst,jbsd->btd", pick, weighted, preferred_element_type=f32).astype(
        bf16
    )
    dresult = (gate_slots * cot_f).astype(bf16)
    dhidden = jnp.einsum("jrd,jfd->jrf", dresult, w_dn, preferred_element_type=f32)
    dgate_val = (dhidden * up_val * sig * (1.0 + gate_val * (1.0 - sig))).astype(bf16)
    dup_val = (dhidden * activated).astype(bf16)
    dboth = jnp.concatenate([dgate_val, dup_val], axis=-1)
    dassign = jnp.einsum("jrf,jdf->jrd", dboth, w_gu, preferred_element_type=f32).astype(bf16)
    dassign = dassign.reshape(2, NE, SLOTS, D)
    drows_part = jnp.einsum("jbst,jbsd->btd", pick, dassign, preferred_element_type=f32)
    dgate_tok = jnp.sum(pick_f * dgate_slots[..., None], axis=2)
    dgate_high = dgate_tok.astype(bf16).astype(f32)
    dgate_low = dgate_tok - dgate_high
    lanes = jnp.arange(128)
    extra_cols = jnp.zeros((NE, LP, 128), f32)
    for j in range(2):
        extra_cols = extra_cols + jnp.where(lanes == 2 * e + j, dgate_high[j][..., None], 0.0)
        extra_cols = extra_cols + jnp.where(
            lanes == EXPERTS + 2 * e + j, dgate_low[j][..., None], 0.0
        )
    drows_send = jnp.concatenate([drows_part, extra_cols], axis=-1).astype(bf16)
    drows = scatter_expert(drows_send)

    grad_gu_part = jnp.einsum("jrd,jrf->jdf", inputs, dboth, preferred_element_type=f32)
    grad_dn_part = jnp.einsum("jrf,jrd->jfd", hidden, dresult, preferred_element_type=f32)
    grad_gu = lax.psum_scatter(
        grad_gu_part.astype(bf16).reshape(2, NF, LP, 2 * FF).swapaxes(0, 1),
        "fsdp",
        scatter_dimension=0,
    ).astype(f32)
    grad_gate, grad_up = grad_gu[..., :FF], grad_gu[..., FF:]
    grad_down = lax.psum_scatter(
        grad_dn_part.astype(bf16).reshape(2, FF, NF, LP).transpose(2, 0, 1, 3),
        "fsdp",
        scatter_dimension=0,
    ).astype(f32)
    mix = scatter_expert(mix_part)
    layer_output = (after_attn + mix).astype(bf16)

    logits = jnp.dot(normed_two, router, preferred_element_type=f32)
    gates = masked_gates(logits, member_own)
    dgate_own = drows[:, D : D + EXPERTS] + drows[:, D + EXPERTS : D + 2 * EXPERTS]
    dlogits = gates * (dgate_own - jnp.sum(gates * dgate_own, axis=-1, keepdims=True))
    dnormed_two = drows[:, :D] + jnp.einsum(
        "te,de->td", dlogits, router.astype(f32), precision=highest
    )
    dafter_norm, part_gain_two = norm_back(dnormed_two, after_attn, gain_two)
    dafter = cot_own.astype(f32) + dafter_norm
    dbranch = dafter.astype(bf16)
    dattended_own = jnp.einsum("td,id->ti", dbranch, w_out, preferred_element_type=f32).astype(
        bf16
    )
    dattended = swap_fsdp(dattended_own.reshape(LP, NF, 128).swapaxes(0, 1)).reshape(
        LENGTH, 2, HEAD_DIM
    )
    dbranch_all = gather_fsdp(dbranch).reshape(LENGTH, D)
    part_router = jnp.einsum(
        "td,te->de", normed_two.astype(f32), dlogits, precision=highest
    )

    dvalue = jnp.einsum("hqk,qhd->kd", probs_low, dattended, preferred_element_type=f32)
    dprobs = jnp.einsum("qhd,kd->hqk", dattended, value, preferred_element_type=f32)
    delta = jnp.sum(probs * dprobs, axis=-1, keepdims=True)
    dscores = (probs * (dprobs - delta)).astype(bf16)
    dquery = jnp.einsum("hqk,kd->qhd", dscores, key, preferred_element_type=f32) * scale
    dkey = jnp.einsum("hqk,qhd->kd", dscores, query, preferred_element_type=f32) * scale
    unrotated = rotate(
        jnp.concatenate([dquery, dkey[:, None]], axis=1), cosine_tab, -sine_tab
    ).reshape(LENGTH, 192)
    dqkv = jnp.concatenate([unrotated, dvalue], axis=-1).astype(bf16)
    part_qkv = jnp.einsum("td,ti->di", normed, dqkv, preferred_element_type=f32)
    dnormed_part = jnp.einsum("ti,di->td", dqkv, w_qkv, preferred_element_type=f32)
    part_gain_one = jnp.sum(dnormed_part * (x_full * r_one), axis=0)
    dnormed = lax.psum_scatter(
        dnormed_part.astype(bf16).reshape(NF, LP, D), "fsdp", scatter_dimension=0
    ).astype(f32)
    dinput_norm, _ = norm_back(dnormed, x_own.astype(f32), gain_one)
    grad_input = (dafter + dinput_norm).astype(bf16)

    part_output = jnp.einsum("ti,td->id", attended, dbranch_all, preferred_element_type=f32)
    grad_output = lax.psum(part_output.astype(bf16), "expert").astype(f32)
    small = jnp.concatenate(
        [
            part_qkv,
            part_router,
            part_gain_one[:, None],
            part_gain_two[:, None],
            jnp.zeros((D, 94), f32),
        ],
        axis=-1,
    ).astype(bf16)
    traded = swap_fsdp(small.reshape(NF, LP, 384))
    heads_part = traded[:, :, :256].swapaxes(0, 1)
    rest_part = jnp.sum(traded[:, :, 256:].astype(f32), axis=0).astype(bf16)
    total_part = jnp.concatenate([heads_part.reshape(LP, 2048), rest_part], axis=-1)
    chunk = lax.all_to_all(
        total_part.reshape(NE, LP // NE, 2176), "expert", split_axis=0, concat_axis=0, tiled=True
    )
    chunk = jnp.sum(chunk.astype(f32), axis=0).astype(bf16)
    total_sum = lax.all_gather(chunk, "expert", axis=0, tiled=True).astype(f32)
    heads_sum = total_sum[:, :2048].reshape(LP, NF, 256)
    grad_query = heads_sum[:, :, :128].reshape(LP, 1024)
    grad_key = heads_sum[:, :, 128:192].reshape(LP, 512)
    grad_value = heads_sum[:, :, 192:].reshape(LP, 512)
    grad_router = total_sum[:, 2048:2080]
    grad_gain_one = total_sum[:, 2080]
    grad_gain_two = total_sum[:, 2081]
    return (
        layer_output[None],
        grad_input[None],
        grad_gain_one,
        grad_query,
        grad_key,
        grad_value,
        grad_output,
        grad_router,
        grad_gain_two,
        grad_gate,
        grad_up,
        grad_down,
    )


def solution(mesh):
    placed = (
        P("expert", "fsdp", None),
        P("expert", None),
        P("expert", "fsdp", None),
        P("fsdp"),
        P("fsdp", None),
        P("fsdp", None),
        P("fsdp", None),
        P("fsdp", None),
        P("fsdp", None),
        P("fsdp"),
        P("expert", "fsdp", None),
        P("expert", "fsdp", None),
        P("expert", None, "fsdp"),
        P("expert", "fsdp", None),
    )
    return jax.shard_map(
        local,
        mesh=mesh,
        in_specs=placed,
        out_specs=(
            P("expert", "fsdp", None),
            P("expert", "fsdp", None),
            P("fsdp"),
            P("fsdp", None),
            P("fsdp", None),
            P("fsdp", None),
            P("fsdp", None),
            P("fsdp", None),
            P("fsdp"),
            P("expert", "fsdp", None),
            P("expert", "fsdp", None),
            P("expert", None, "fsdp"),
        ),
        check_vma=False,
    )
```

```python
import jax
import jax.numpy as jnp
from jax import lax
from jax.experimental import pallas as pl
from jax.experimental.pallas import tpu as pltpu
from jax.sharding import PartitionSpec as P

HEAD_DIM = 64
EXPERTS = 32
SLOTS = 64
NF = 8
NE = 16
LP = 128
LENGTH = 1024
D = 1024
FF = 512

epsilon = 1e-06
rope_base = 10000.0
highest = lax.Precision.HIGHEST
bf16 = jnp.bfloat16
f32 = jnp.float32


def shift_x(v, k):
    return lax.ppermute(v, "fsdp", [(i, (i + 2 * k) % NF) for i in range(NF)])


def swap_core(v):
    return lax.ppermute(v, "fsdp", [(i, i ^ 1) for i in range(NF)])


def shift_z(v, k):
    return lax.ppermute(v, "expert", [(i, (i // 4) * 4 + (i + k) % 4) for i in range(NE)])


def shift_y(v, k):
    return lax.ppermute(v, "expert", [(i, (i + 4 * k) % NE) for i in range(NE)])


def put(buffer, piece, place):
    return lax.dynamic_update_index_in_dim(buffer, piece, place, 0)


def ring_gather(shift, v, place):
    got = [(v, place)] + [(shift(v, k), (place - k) % 4) for k in (1, 3, 2)]
    out = jnp.zeros((4,) + v.shape, v.dtype)
    for piece, where in got:
        out = put(out, piece, where)
    return out


def gather_fsdp(v):
    f = lax.axis_index("fsdp")
    x, c = f // 2, f % 2
    mine = ring_gather(shift_x, v, x)
    other = swap_core(mine)
    first = jnp.where(c == 0, mine, other)
    second = jnp.where(c == 0, other, mine)
    return jnp.stack([first, second], axis=1).reshape((NF,) + v.shape)


def gather_expert(v):
    e = lax.axis_index("expert")
    y, z = e // 4, e % 4
    n = v.shape[0] // 2
    a = ring_gather(shift_z, v[:n], z)
    b = ring_gather(shift_y, v[n:], y)
    a = ring_gather(shift_y, a, y)
    b = ring_gather(shift_z, b, z)
    return jnp.concatenate([a, jnp.swapaxes(b, 0, 1)], axis=2).reshape((NE,) + v.shape)


def ring_sum(shift, p, place):
    total = lax.dynamic_index_in_dim(p, place, 0, keepdims=False).astype(f32)
    for k in (1, 3, 2):
        piece = lax.dynamic_index_in_dim(p, (place + k) % 4, 0, keepdims=False)
        total = total + shift(piece, k).astype(f32)
    return total


def scatter_expert(p, beside=None):
    e = lax.axis_index("expert")
    y, z = e // 4, e % 4
    n = p.shape[1] // 2
    p = p.reshape((4, 4) + p.shape[1:])
    a = p[:, :, :n]
    b = jnp.swapaxes(p[:, :, n:], 0, 1)
    a = ring_sum(shift_y, a, y).astype(bf16)
    b = ring_sum(shift_z, b, z).astype(bf16)
    if beside is not None:
        a, b, beside = lax.optimization_barrier((a, b, beside))
    a = ring_sum(shift_z, a, z)
    b = ring_sum(shift_y, b, y)
    return jnp.concatenate([a, b], axis=0), beside


def after(v, first):
    return lax.optimization_barrier((v, first))[0]


def dot(a, b, dims=((1,), (0,))):
    return lax.dot_general(a, b, (dims, ((), ())), preferred_element_type=f32)


NT = ((1,), (1,))
TN = ((0,), (0,))


def expert_kernel(
    e_ref, rows, cot, member, pick, pick_t, router, w, inputs, hidden, dboth, dres, mix, drows
):
    e = e_ref[0]
    lane = lax.broadcasted_iota(jnp.int32, (1, 128), 1)
    gates = []
    for b in range(4):
        has = member[b] > 0
        low = jnp.where(has, dot(rows[b], router[...]), -1e30)
        top = jnp.max(low, axis=-1, keepdims=True)
        expo = jnp.where(has, jnp.exp(low - top), 0.0)
        soft = expo / jnp.sum(expo, axis=-1, keepdims=True)
        high = soft.astype(bf16)
        rest = soft - high.astype(f32)
        mid = rest.astype(bf16)
        last = (rest - mid.astype(f32)).astype(bf16)
        gates.append(dot(pick[b], high) + dot(pick[b], mid) + dot(pick[b], last))
    x_slots = [dot(pick[b], rows[b]).astype(bf16) for b in range(4)]
    c_slots = [dot(pick[b], cot[b, :LP]) for b in range(4)]
    weighted, dassign, extra = [], [], []
    for j in range(2):
        part = slice(j * SLOTS, (j + 1) * SLOTS)
        x_in = jnp.concatenate([v[part] for v in x_slots], axis=0)
        c_in = jnp.concatenate([v[part] for v in c_slots], axis=0)
        gate_rows = jnp.concatenate([v[part] for v in gates], axis=0)
        gate_in = jnp.sum(jnp.where(lane == 2 * e + j, gate_rows, 0.0), axis=-1, keepdims=True)
        w_g = w[:, j * 1024 : j * 1024 + FF]
        w_u = w[:, j * 1024 + FF : (j + 1) * 1024]
        w_d = w[:, 2048 + j * FF : 2048 + (j + 1) * FF]
        gate_val = dot(x_in, w_g)
        up_val = dot(x_in, w_u)
        sig = 1.0 / (1.0 + jnp.exp(-gate_val))
        activated = gate_val * sig
        hid = (activated * up_val).astype(bf16)
        result = dot(hid, w_d, NT).astype(bf16).astype(f32)
        dgate = jnp.sum(result * c_in, axis=-1, keepdims=True)
        dresult = (gate_in * c_in).astype(bf16)
        dhidden = dot(dresult, w_d)
        dgate_val = (dhidden * up_val * sig * (1.0 + gate_val * (1.0 - sig))).astype(bf16)
        dup_val = (dhidden * activated).astype(bf16)
        da = (dot(dgate_val, w_g, NT) + dot(dup_val, w_u, NT)).astype(bf16)
        weighted.append((gate_in * result).astype(bf16))
        dassign.append(da)
        dg_high = dgate.astype(bf16).astype(f32)
        dg_low = dgate - dg_high
        extra.append(
            (
                jnp.where(lane == 2 * e + j, dg_high, 0.0)
                + jnp.where(lane == EXPERTS + 2 * e + j, dg_low, 0.0)
            ).astype(bf16)
        )
        inputs[j] = x_in
        hidden[j] = hid
        dboth[j, :, :FF] = dgate_val
        dboth[j, :, FF:] = dup_val
        dres[j] = dresult
    for b in range(4):
        part = slice(b * SLOTS, (b + 1) * SLOTS)
        mix[b] = dot(
            pick_t[b], jnp.concatenate([weighted[0][part], weighted[1][part]], axis=0)
        ).astype(bf16)
        drows[b, :, :D] = dot(
            pick_t[b], jnp.concatenate([dassign[0][part], dassign[1][part]], axis=0)
        ).astype(bf16)
        drows[b, :, D:] = dot(
            pick_t[b], jnp.concatenate([extra[0][part], extra[1][part]], axis=0)
        ).astype(bf16)


def experts(e, rows_all, cot_all, member, pick, pick_t, router, w):
    rows = NE * SLOTS
    step = rows // 4
    return pl.pallas_call(
        expert_kernel,
        grid=(4,),
        in_specs=[
            pl.BlockSpec(memory_space=pltpu.SMEM),
            pl.BlockSpec((4, LP, D), lambda i: (i, 0, 0)),
            pl.BlockSpec((4, cot_all.shape[1], D), lambda i: (i, 0, 0)),
            pl.BlockSpec((4, LP, 128), lambda i: (i, 0, 0)),
            pl.BlockSpec((4, 128, LP), lambda i: (i, 0, 0)),
            pl.BlockSpec((4, LP, 128), lambda i: (i, 0, 0)),
            pl.BlockSpec((D, 128), lambda i: (0, 0)),
            pl.BlockSpec((D, 3072), lambda i: (0, 0), pipeline_mode=pl.Buffered(1)),
        ],
        out_specs=[
            pl.BlockSpec((2, step, D), lambda i: (0, i, 0)),
            pl.BlockSpec((2, step, FF), lambda i: (0, i, 0)),
            pl.BlockSpec((2, step, 2 * FF), lambda i: (0, i, 0)),
            pl.BlockSpec((2, step, D), lambda i: (0, i, 0)),
            pl.BlockSpec((4, LP, D), lambda i: (i, 0, 0)),
            pl.BlockSpec((4, LP, D + 128), lambda i: (i, 0, 0)),
        ],
        out_shape=[
            jax.ShapeDtypeStruct((2, rows, D), bf16),
            jax.ShapeDtypeStruct((2, rows, FF), bf16),
            jax.ShapeDtypeStruct((2, rows, 2 * FF), bf16),
            jax.ShapeDtypeStruct((2, rows, D), bf16),
            jax.ShapeDtypeStruct((NE, LP, D), bf16),
            jax.ShapeDtypeStruct((NE, LP, D + 128), bf16),
        ],
        compiler_params=pltpu.CompilerParams(vmem_limit_bytes=56 * 2**20),
        cost_estimate=pl.CostEstimate(
            flops=14 * 10**9, bytes_accessed=30 * 2**20, transcendentals=10**6
        ),
        name="experts",
    )(e, rows_all, cot_all, member, pick, pick_t, router, w)


def weight_kernel(inputs, dres, dboth, hidden, out):
    for j in range(2):
        out[:, j * 1024 : (j + 1) * 1024] = dot(inputs[j], dboth[j], TN).astype(bf16)
        out[:, 2048 + j * FF : 2048 + (j + 1) * FF] = dot(dres[j], hidden[j], TN).astype(bf16)


def expert_weights(inputs, dres, dboth, hidden):
    rows = NE * SLOTS
    return pl.pallas_call(
        weight_kernel,
        grid=(4,),
        in_specs=[
            pl.BlockSpec((2, rows, 256), lambda i: (0, 0, i)),
            pl.BlockSpec((2, rows, 256), lambda i: (0, 0, i)),
            pl.BlockSpec((2, rows, 2 * FF), lambda i: (0, 0, 0)),
            pl.BlockSpec((2, rows, FF), lambda i: (0, 0, 0)),
        ],
        out_specs=pl.BlockSpec((256, 3072), lambda i: (i, 0)),
        out_shape=jax.ShapeDtypeStruct((D, 3072), bf16),
        compiler_params=pltpu.CompilerParams(vmem_limit_bytes=56 * 2**20),
        cost_estimate=pl.CostEstimate(
            flops=7 * 10**9, bytes_accessed=20 * 2**20, transcendentals=0
        ),
        name="expert_weights",
    )(inputs, dres, dboth, hidden)


def swap_fsdp(v):
    return lax.all_to_all(v, "fsdp", split_axis=0, concat_axis=0, tiled=True)


def rope_tables(positions):
    half_width = HEAD_DIM // 2
    exponent = jnp.arange(half_width).astype(f32) * (2.0 / HEAD_DIM)
    inverse = rope_base ** (-exponent)
    angles = positions.astype(f32)[:, None] * inverse[None, :]
    return (jnp.cos(angles), jnp.sin(angles))


def rotate(vectors, cosine_tab, sine_tab):
    a, b = vectors[..., : HEAD_DIM // 2], vectors[..., HEAD_DIM // 2 :]
    cos, sin = cosine_tab[:, None, :], sine_tab[:, None, :]
    return jnp.concatenate([a * cos - b * sin, b * cos + a * sin], axis=-1)


def masked_gates(logits, member):
    low = jnp.where(member, logits, -1e30)
    top = jnp.max(low, axis=-1, keepdims=True)
    expo = jnp.where(member, jnp.exp(low - top), 0.0)
    return expo / jnp.sum(expo, axis=-1, keepdims=True)


def norm_back(u, v, gain):
    r = lax.rsqrt(jnp.mean(v * v, axis=-1, keepdims=True) + epsilon)
    inner = jnp.mean(gain * u * v, axis=-1, keepdims=True)
    return r * gain * u - v * (r * r * r) * inner, jnp.sum(u * v * r, axis=0)


def local(
    layer_input,
    segment_ids,
    routes,
    attn_gain,
    w_query,
    w_key,
    w_value,
    w_output,
    w_router,
    ffn_gain,
    w_gate,
    w_up,
    w_down,
    cotangent,
):
    e = lax.axis_index("expert")
    x_own = layer_input[0]
    cot_own = cotangent[0]
    columns = jnp.concatenate(
        [
            w_query.reshape(LP, NF, 128),
            w_key.reshape(LP, NF, 64),
            w_value.reshape(LP, NF, 64),
        ],
        axis=-1,
    ).swapaxes(0, 1)
    extra = jnp.concatenate(
        [
            jnp.concatenate([attn_gain, ffn_gain])[None],
            w_router.reshape(16, 256),
            jnp.zeros((15, 256), bf16),
        ],
        axis=0,
    )
    payload = jnp.concatenate([columns, jnp.broadcast_to(extra[None], (NF, 32, 256))], axis=1)
    x_all = lax.all_gather(x_own, "fsdp", axis=0, tiled=True)
    got = swap_fsdp(payload)
    w_qkv = got[:, :LP].reshape(D, 256)
    gain_one = got[:, LP, :128].reshape(D).astype(f32)
    gain_two = got[:, LP, 128:].reshape(D).astype(f32)
    router = got[:, LP + 1 : LP + 17].reshape(D, EXPERTS)
    w_out = lax.all_gather(after(w_output, x_all), "fsdp", axis=0, tiled=True)
    w_own = jnp.concatenate(
        [w_gate[0], w_up[0], w_gate[1], w_up[1], w_down[0].T, w_down[1].T], axis=1
    )
    w_exp = lax.all_gather(after(w_own, w_out), "fsdp", axis=0, tiled=True)
    cot_all = gather_expert(
        jnp.concatenate(
            [cot_own, routes[0].astype(bf16).reshape(1, D), jnp.zeros((15, D), bf16)], axis=0
        )
    )
    routes_all = cot_all[:, LP].reshape(NE, LP, 8).astype(jnp.int32)

    own_ids = 2 * e + jnp.arange(2, dtype=jnp.int32)
    chosen_own = jnp.any(routes_all[:, :, :, None] == own_ids, axis=2)
    before = (jnp.arange(LP)[:, None] > jnp.arange(LP)[None, :]).astype(bf16)
    rank = jnp.einsum(
        "ts,bsj->bjt", before, chosen_own.astype(bf16), preferred_element_type=f32
    )
    slot_ids = jnp.arange(SLOTS, dtype=f32)
    member_t = chosen_own.swapaxes(1, 2)
    pick = (
        ((rank[:, :, None, :] == slot_ids[:, None]) & member_t[:, :, None, :])
        .astype(bf16)
        .reshape(NE, 2 * SLOTS, LP)
    )
    pick_t = pick.swapaxes(1, 2)
    member_all = jnp.any(
        routes_all[:, :, :, None] == jnp.arange(128, dtype=jnp.int32), axis=2
    ).astype(bf16)
    member_own = jnp.any(
        routes[0][:, :, None] == jnp.arange(EXPERTS, dtype=jnp.int32), axis=1
    )
    router_wide = jnp.concatenate([router, jnp.zeros((D, 128 - EXPERTS), bf16)], axis=1)

    x_full = x_all.astype(f32)
    r_one = lax.rsqrt(jnp.mean(x_full * x_full, axis=-1, keepdims=True) + epsilon)
    normed = (x_full * r_one * gain_one).astype(bf16)
    qkv = jnp.dot(normed, w_qkv, preferred_element_type=f32)
    cosine_tab, sine_tab = rope_tables(jnp.arange(LENGTH))
    rotated = rotate(qkv[:, :192].reshape(LENGTH, 3, HEAD_DIM), cosine_tab, sine_tab).astype(bf16)
    query, key = rotated[:, :2], rotated[:, 2]
    value = qkv[:, 192:].astype(bf16)
    seg = segment_ids[0]
    places = jnp.arange(LENGTH)
    allowed = (seg[:, None] == seg[None, :]) & (places[None, :] <= places[:, None])
    scale = HEAD_DIM**-0.5
    scores = jnp.einsum("qhd,kd->hqk", query, key, preferred_element_type=f32) * scale
    scores = jnp.where(allowed, scores, -1e30)
    row_top = jnp.max(scores, axis=-1, keepdims=True)
    expo = jnp.exp(scores - row_top)
    total = jnp.sum(expo, axis=-1, keepdims=True)
    probs = expo / total
    probs_low = probs.astype(bf16)
    attended = jnp.einsum("hqk,kd->qhd", probs_low, value, preferred_element_type=f32)
    attended = attended.reshape(LENGTH, 128).astype(bf16)
    attended_own = swap_fsdp(attended.reshape(NF, LP, 128)).swapaxes(0, 1).reshape(LP, D)
    after_attn = x_own.astype(f32) + jnp.dot(attended_own, w_out, preferred_element_type=f32)
    r_two = lax.rsqrt(jnp.mean(after_attn * after_attn, axis=-1, keepdims=True) + epsilon)
    normed_two = (after_attn * r_two * gain_two).astype(bf16)

    rows_all = gather_expert(normed_two)
    inputs, hidden, dboth, dres, mix_part, drows_part = experts(
        e[None], rows_all, cot_all, member_all, pick, pick_t, router_wide, w_exp
    )
    grad_exp = expert_weights(inputs, dres, dboth, hidden)
    drows, grad_exp = scatter_expert(drows_part, grad_exp)
    grad_exp = lax.psum_scatter(
        grad_exp.reshape(NF, LP, 3072), "fsdp", scatter_dimension=0
    ).astype(f32)
    grad_gate = jnp.stack([grad_exp[:, :512], grad_exp[:, 1024:1536]])
    grad_up = jnp.stack([grad_exp[:, 512:1024], grad_exp[:, 1536:2048]])
    grad_down = jnp.stack([grad_exp[:, 2048:2560].T, grad_exp[:, 2560:].T])
    mix, _ = scatter_expert(after(mix_part, drows))
    layer_output = (after_attn + mix).astype(bf16)

    logits = jnp.dot(normed_two, router, preferred_element_type=f32)
    gates = masked_gates(logits, member_own)
    dgate_own = drows[:, D : D + EXPERTS] + drows[:, D + EXPERTS : D + 2 * EXPERTS]
    dlogits = gates * (dgate_own - jnp.sum(gates * dgate_own, axis=-1, keepdims=True))
    dnormed_two = drows[:, :D] + jnp.einsum(
        "te,de->td", dlogits, router.astype(f32), precision=highest
    )
    dafter_norm, part_gain_two = norm_back(dnormed_two, after_attn, gain_two)
    dafter = cot_own.astype(f32) + dafter_norm
    dbranch = dafter.astype(bf16)
    dattended_own = jnp.einsum("td,id->ti", dbranch, w_out, preferred_element_type=f32).astype(
        bf16
    )
    dattended = swap_fsdp(dattended_own.reshape(LP, NF, 128).swapaxes(0, 1)).reshape(
        LENGTH, 2, HEAD_DIM
    )
    dbranch_all = lax.all_gather(dbranch, "fsdp", axis=0, tiled=True)
    part_router = jnp.einsum(
        "td,te->de", normed_two.astype(f32), dlogits, precision=highest
    )

    dvalue = jnp.einsum("hqk,qhd->kd", probs_low, dattended, preferred_element_type=f32)
    dprobs = jnp.einsum("qhd,kd->hqk", dattended, value, preferred_element_type=f32)
    delta = jnp.sum(probs * dprobs, axis=-1, keepdims=True)
    dscores = (probs * (dprobs - delta)).astype(bf16)
    dquery = jnp.einsum("hqk,kd->qhd", dscores, key, preferred_element_type=f32) * scale
    dkey = jnp.einsum("hqk,qhd->kd", dscores, query, preferred_element_type=f32) * scale
    unrotated = rotate(
        jnp.concatenate([dquery, dkey[:, None]], axis=1), cosine_tab, -sine_tab
    ).reshape(LENGTH, 192)
    dqkv = jnp.concatenate([unrotated, dvalue], axis=-1).astype(bf16)
    part_qkv = jnp.einsum("td,ti->di", normed, dqkv, preferred_element_type=f32)
    dnormed_part = jnp.einsum("ti,di->td", dqkv, w_qkv, preferred_element_type=f32)
    part_gain_one = jnp.sum(dnormed_part * (x_full * r_one), axis=0)
    dnormed = lax.psum_scatter(
        dnormed_part.astype(bf16).reshape(NF, LP, D), "fsdp", scatter_dimension=0
    ).astype(f32)
    dinput_norm, _ = norm_back(dnormed, x_own.astype(f32), gain_one)
    grad_input = (dafter + dinput_norm).astype(bf16)

    part_output = jnp.einsum("ti,td->id", attended, dbranch_all, preferred_element_type=f32)
    part_output = lax.all_to_all(
        part_output.astype(bf16).reshape(NE, LP // NE, D),
        "expert",
        split_axis=0,
        concat_axis=0,
        tiled=True,
    )
    chunk_output = jnp.sum(part_output.astype(f32), axis=0)
    small = jnp.concatenate(
        [
            part_qkv,
            part_router,
            part_gain_one[:, None],
            part_gain_two[:, None],
            jnp.zeros((D, 94), f32),
        ],
        axis=-1,
    ).astype(bf16)
    small = small.reshape(NF, NE, LP // NE, 384).swapaxes(0, 1).reshape(NF * NE, LP // NE, 384)
    small = lax.all_to_all(small, ("expert", "fsdp"), split_axis=0, concat_axis=0, tiled=True)
    small = jnp.sum(small.reshape(NE, NF, LP // NE, 384).astype(f32), axis=0)
    chunk = jnp.concatenate(
        [
            small[:, :, :256].swapaxes(0, 1).reshape(LP // NE, 2048),
            jnp.sum(small[:, :, 256:], axis=0),
            chunk_output,
        ],
        axis=-1,
    ).astype(bf16)
    total_sum = lax.all_to_all(
        jnp.broadcast_to(chunk[None], (NE,) + chunk.shape),
        "expert",
        split_axis=0,
        concat_axis=0,
        tiled=True,
    ).reshape(LP, 3200)
    total_sum = total_sum.astype(f32)
    heads_sum = total_sum[:, :2048].reshape(LP, NF, 256)
    grad_output = total_sum[:, 2176:]
    grad_query = heads_sum[:, :, :128].reshape(LP, 1024)
    grad_key = heads_sum[:, :, 128:192].reshape(LP, 512)
    grad_value = heads_sum[:, :, 192:].reshape(LP, 512)
    grad_router = total_sum[:, 2048:2080]
    grad_gain_one = total_sum[:, 2080]
    grad_gain_two = total_sum[:, 2081]
    return (
        layer_output[None],
        grad_input[None],
        grad_gain_one,
        grad_query,
        grad_key,
        grad_value,
        grad_output,
        grad_router,
        grad_gain_two,
        grad_gate,
        grad_up,
        grad_down,
    )


def solution(mesh):
    placed = (
        P("expert", "fsdp", None),
        P("expert", None),
        P("expert", "fsdp", None),
        P("fsdp"),
        P("fsdp", None),
        P("fsdp", None),
        P("fsdp", None),
        P("fsdp", None),
        P("fsdp", None),
        P("fsdp"),
        P("expert", "fsdp", None),
        P("expert", "fsdp", None),
        P("expert", None, "fsdp"),
        P("expert", "fsdp", None),
    )
    return jax.shard_map(
        local,
        mesh=mesh,
        in_specs=placed,
        out_specs=(
            P("expert", "fsdp", None),
            P("expert", "fsdp", None),
            P("fsdp"),
            P("fsdp", None),
            P("fsdp", None),
            P("fsdp", None),
            P("fsdp", None),
            P("fsdp", None),
            P("fsdp"),
            P("expert", "fsdp", None),
            P("expert", "fsdp", None),
            P("expert", None, "fsdp"),
        ),
        check_vma=False,
    )
```

```python
import jax
import jax.numpy as jnp
import numpy as np
from jax import lax
from jax.experimental import pallas as pl
from jax.experimental.pallas import tpu as pltpu
from jax.sharding import PartitionSpec as P

HEAD_DIM = 64
EXPERTS = 32
SLOTS = 64
NF = 8
NE = 16
LP = 128
LENGTH = 1024
D = 1024
FF = 512

epsilon = 1e-06
rope_base = 10000.0
highest = lax.Precision.HIGHEST
bf16 = jnp.bfloat16
f32 = jnp.float32


def shift_x(v, k):
    return lax.ppermute(v, "fsdp", [(i, (i + 2 * k) % NF) for i in range(NF)])


def swap_core(v):
    return lax.ppermute(v, "fsdp", [(i, i ^ 1) for i in range(NF)])


def shift_z(v, k):
    return lax.ppermute(v, "expert", [(i, (i // 4) * 4 + (i + k) % 4) for i in range(NE)])


def shift_y(v, k):
    return lax.ppermute(v, "expert", [(i, (i + 4 * k) % NE) for i in range(NE)])


def put(buffer, piece, place):
    return lax.dynamic_update_index_in_dim(buffer, piece, place, 0)


def ring_gather(shift, v, place):
    got = [(v, place)] + [(shift(v, k), (place - k) % 4) for k in (1, 3, 2)]
    out = jnp.zeros((4,) + v.shape, v.dtype)
    for piece, where in got:
        out = put(out, piece, where)
    return out


def ring_gather_halves(shift, v, place):
    left, right = shift(v, 1), shift(v, 3)
    n = v.shape[0] // 2
    far = (shift(left[:n], 1), shift(right[n:], 3))
    out = jnp.zeros((4,) + v.shape, v.dtype)
    for piece, where in ((v, place), (left, (place - 1) % 4), (right, (place + 1) % 4)):
        out = put(out, piece, where)
    return put(out, jnp.concatenate(far, axis=0), (place + 2) % 4)


def gather_fsdp(v, beside=None):
    f = lax.axis_index("fsdp")
    x, c = f // 2, f % 2
    mine = ring_gather(shift_x, v, x)
    if beside is not None:
        mine, beside = lax.optimization_barrier((mine, beside))
    other = swap_core(mine)
    first = jnp.where(c == 0, mine, other)
    second = jnp.where(c == 0, other, mine)
    return jnp.stack([first, second], axis=1).reshape((NF,) + v.shape), beside


def gather_expert(v, beside):
    e = lax.axis_index("expert")
    y, z = e // 4, e % 4
    n = v.shape[0] // 2
    a = ring_gather(shift_z, v[:n], z)
    b = ring_gather(shift_y, v[n:], y)
    a, b, beside = lax.optimization_barrier((a, b, beside))
    a = ring_gather_halves(shift_y, a, y)
    b = ring_gather_halves(shift_z, b, z)
    whole = jnp.concatenate([a, jnp.swapaxes(b, 0, 1)], axis=2).reshape((NE,) + v.shape)
    return whole, beside


def pieces_of(p, place):
    return [
        lax.dynamic_index_in_dim(p, (place + k) % 4, 0, keepdims=False) for k in range(4)
    ]


def ring_sum(shift, p, place):
    own, *others = pieces_of(p, place)
    total = own.astype(f32)
    for k in (1, 3, 2):
        total = total + shift(others[k - 1], k).astype(f32)
    return total


def ring_sum_halves(shift, p, place):
    own, right, far, left = pieces_of(p, place)
    n = own.shape[0] // 2
    from_left, from_right = shift(far[:n], 1), shift(far[n:], 3)
    right = jnp.concatenate([right[:n].astype(f32) + from_left.astype(f32), right[n:]], axis=0)
    left = jnp.concatenate([left[:n], left[n:].astype(f32) + from_right.astype(f32)], axis=0)
    total = own.astype(f32) + shift(right.astype(bf16), 1).astype(f32)
    return total + shift(left.astype(bf16), 3).astype(f32)


def scatter_expert(p, beside):
    e = lax.axis_index("expert")
    y, z = e // 4, e % 4
    n = p.shape[1] // 2
    p = p.reshape((4, 4) + p.shape[1:])
    a = p[:, :, :n]
    b = jnp.swapaxes(p[:, :, n:], 0, 1)
    a = ring_sum_halves(shift_y, a, y).astype(bf16)
    b = ring_sum_halves(shift_z, b, z).astype(bf16)
    a, b, beside = lax.optimization_barrier((a, b, beside))
    a = ring_sum(shift_z, a, z)
    b = ring_sum(shift_y, b, y)
    return jnp.concatenate([a, b], axis=0), beside


def after(v, first):
    return lax.optimization_barrier((v, first))[0]


def dot(a, b, dims=((1,), (0,))):
    return lax.dot_general(a, b, (dims, ((), ())), preferred_element_type=f32)


NT = ((1,), (1,))
TN = ((0,), (0,))


def expert_kernel(
    e_ref, rows, cot, member, pick, pick_t, router, w, inputs, hidden, dboth, dres, mix, drows
):
    e = e_ref[0]
    lane = lax.broadcasted_iota(jnp.int32, (1, 128), 1)
    gates = []
    for b in range(4):
        has = member[b] > 0
        low = jnp.where(has, dot(rows[b], router[...]), -1e30)
        top = jnp.max(low, axis=-1, keepdims=True)
        expo = jnp.where(has, jnp.exp(low - top), 0.0)
        soft = expo / jnp.sum(expo, axis=-1, keepdims=True)
        high = soft.astype(bf16)
        rest = soft - high.astype(f32)
        mid = rest.astype(bf16)
        last = (rest - mid.astype(f32)).astype(bf16)
        gates.append(dot(pick[b], high) + dot(pick[b], mid) + dot(pick[b], last))
    x_slots = [dot(pick[b], rows[b]).astype(bf16) for b in range(4)]
    c_slots = [dot(pick[b], cot[b, :LP]) for b in range(4)]
    weighted, dassign, extra = [], [], []
    for j in range(2):
        part = slice(j * SLOTS, (j + 1) * SLOTS)
        x_in = jnp.concatenate([v[part] for v in x_slots], axis=0)
        c_in = jnp.concatenate([v[part] for v in c_slots], axis=0)
        gate_rows = jnp.concatenate([v[part] for v in gates], axis=0)
        gate_in = jnp.sum(jnp.where(lane == 2 * e + j, gate_rows, 0.0), axis=-1, keepdims=True)
        w_g = w[:, j * 1024 : j * 1024 + FF]
        w_u = w[:, j * 1024 + FF : (j + 1) * 1024]
        w_d = w[:, 2048 + j * FF : 2048 + (j + 1) * FF]
        gate_val = dot(x_in, w_g)
        up_val = dot(x_in, w_u)
        sig = 1.0 / (1.0 + jnp.exp(-gate_val))
        activated = gate_val * sig
        hid = (activated * up_val).astype(bf16)
        result = dot(hid, w_d, NT).astype(bf16).astype(f32)
        dgate = jnp.sum(result * c_in, axis=-1, keepdims=True)
        dresult = (gate_in * c_in).astype(bf16)
        dhidden = dot(dresult, w_d)
        dgate_val = (dhidden * up_val * sig * (1.0 + gate_val * (1.0 - sig))).astype(bf16)
        dup_val = (dhidden * activated).astype(bf16)
        da = (dot(dgate_val, w_g, NT) + dot(dup_val, w_u, NT)).astype(bf16)
        weighted.append((gate_in * result).astype(bf16))
        dassign.append(da)
        dg_high = dgate.astype(bf16).astype(f32)
        dg_low = dgate - dg_high
        extra.append(
            (
                jnp.where(lane == 2 * e + j, dg_high, 0.0)
                + jnp.where(lane == EXPERTS + 2 * e + j, dg_low, 0.0)
            ).astype(bf16)
        )
        inputs[j] = x_in
        hidden[j] = hid
        dboth[j, :, :FF] = dgate_val
        dboth[j, :, FF:] = dup_val
        dres[j] = dresult
    for b in range(4):
        part = slice(b * SLOTS, (b + 1) * SLOTS)
        mix[b] = dot(
            pick_t[b], jnp.concatenate([weighted[0][part], weighted[1][part]], axis=0)
        ).astype(bf16)
        drows[b, :, :D] = dot(
            pick_t[b], jnp.concatenate([dassign[0][part], dassign[1][part]], axis=0)
        ).astype(bf16)
        drows[b, :, D:] = dot(
            pick_t[b], jnp.concatenate([extra[0][part], extra[1][part]], axis=0)
        ).astype(bf16)


def experts(e, rows_all, cot_all, member, pick, pick_t, router, w):
    rows = NE * SLOTS
    step = rows // 4
    return pl.pallas_call(
        expert_kernel,
        grid=(4,),
        in_specs=[
            pl.BlockSpec(memory_space=pltpu.SMEM),
            pl.BlockSpec((4, LP, D), lambda i: (i, 0, 0)),
            pl.BlockSpec((4, cot_all.shape[1], D), lambda i: (i, 0, 0)),
            pl.BlockSpec((4, LP, 128), lambda i: (i, 0, 0)),
            pl.BlockSpec((4, 128, LP), lambda i: (i, 0, 0)),
            pl.BlockSpec((4, LP, 128), lambda i: (i, 0, 0)),
            pl.BlockSpec((D, 128), lambda i: (0, 0)),
            pl.BlockSpec((D, 3072), lambda i: (0, 0), pipeline_mode=pl.Buffered(1)),
        ],
        out_specs=[
            pl.BlockSpec((2, step, D), lambda i: (0, i, 0)),
            pl.BlockSpec((2, step, FF), lambda i: (0, i, 0)),
            pl.BlockSpec((2, step, 2 * FF), lambda i: (0, i, 0)),
            pl.BlockSpec((2, step, D), lambda i: (0, i, 0)),
            pl.BlockSpec((4, LP, D), lambda i: (i, 0, 0)),
            pl.BlockSpec((4, LP, D + 128), lambda i: (i, 0, 0)),
        ],
        out_shape=[
            jax.ShapeDtypeStruct((2, rows, D), bf16),
            jax.ShapeDtypeStruct((2, rows, FF), bf16),
            jax.ShapeDtypeStruct((2, rows, 2 * FF), bf16),
            jax.ShapeDtypeStruct((2, rows, D), bf16),
            jax.ShapeDtypeStruct((NE, LP, D), bf16),
            jax.ShapeDtypeStruct((NE, LP, D + 128), bf16),
        ],
        compiler_params=pltpu.CompilerParams(vmem_limit_bytes=56 * 2**20),
        cost_estimate=pl.CostEstimate(
            flops=14 * 10**9, bytes_accessed=30 * 2**20, transcendentals=10**6
        ),
        name="experts",
    )(e, rows_all, cot_all, member, pick, pick_t, router, w)


def weight_kernel(inputs, dres, dboth, hidden, out):
    for j in range(2):
        out[:, :, j * 1024 : (j + 1) * 1024] = (
            dot(inputs[j], dboth[j], TN).astype(bf16).reshape(2, LP, 1024)
        )
        out[:, :, 2048 + j * FF : 2048 + (j + 1) * FF] = (
            dot(dres[j], hidden[j], TN).astype(bf16).reshape(2, LP, FF)
        )


def expert_weights(inputs, dres, dboth, hidden):
    rows = NE * SLOTS
    return pl.pallas_call(
        weight_kernel,
        grid=(4,),
        in_specs=[
            pl.BlockSpec((2, rows, 256), lambda i: (0, 0, i)),
            pl.BlockSpec((2, rows, 256), lambda i: (0, 0, i)),
            pl.BlockSpec((2, rows, 2 * FF), lambda i: (0, 0, 0)),
            pl.BlockSpec((2, rows, FF), lambda i: (0, 0, 0)),
        ],
        out_specs=pl.BlockSpec((2, LP, 3072), lambda i: (i, 0, 0)),
        out_shape=jax.ShapeDtypeStruct((NF, LP, 3072), bf16),
        compiler_params=pltpu.CompilerParams(vmem_limit_bytes=56 * 2**20),
        cost_estimate=pl.CostEstimate(
            flops=7 * 10**9, bytes_accessed=20 * 2**20, transcendentals=0
        ),
        name="expert_weights",
    )(inputs, dres, dboth, hidden)


def swap_fsdp(v):
    return lax.all_to_all(v, "fsdp", split_axis=0, concat_axis=0, tiled=True)


def rope_tables():
    exponent = np.arange(HEAD_DIM // 2, dtype=np.float32) * np.float32(2.0 / HEAD_DIM)
    inverse = np.power(np.float32(rope_base), -exponent).astype(np.float32)
    angles = np.arange(LENGTH, dtype=np.float32)[:, None] * inverse[None, :]
    wide = np.tile(angles.astype(np.float32), (1, 4))
    return np.cos(wide).astype(np.float32), np.sin(wide).astype(np.float32)


def masked_gates(logits, member):
    low = jnp.where(member, logits, -1e30)
    top = jnp.max(low, axis=-1, keepdims=True)
    expo = jnp.where(member, jnp.exp(low - top), 0.0)
    return expo / jnp.sum(expo, axis=-1, keepdims=True)


def norm_back(u, v, gain):
    r = lax.rsqrt(jnp.mean(v * v, axis=-1, keepdims=True) + epsilon)
    inner = jnp.mean(gain * u * v, axis=-1, keepdims=True)
    return r * gain * u - v * (r * r * r) * inner, jnp.sum(u * v * r, axis=0)


def masked_scores(q_h, keys, seg_col, seg_row, first):
    rows, count = q_h.shape[0], keys.shape[0]
    scores = dot(q_h, keys, NT) * HEAD_DIM**-0.5
    row = lax.broadcasted_iota(jnp.int32, (rows, count), 0) + first
    column = lax.broadcasted_iota(jnp.int32, (rows, count), 1)
    allowed = (seg_col == seg_row) & (column <= row)
    return jnp.where(allowed, scores, -1e30)


QB = 256


def attend_kernel(x, gain, w, cos, sin, seg_col, seg_row, normed, qkv, attended, lse):
    x_full = x[...].astype(f32)
    r = lax.rsqrt(jnp.mean(x_full * x_full, axis=-1, keepdims=True) + epsilon)
    normed[...] = (x_full * r * gain[...]).astype(bf16)
    raw = dot(normed[...], w[...])
    turned = lax.broadcasted_iota(jnp.int32, (1, 128), 1) < HEAD_DIM
    cos_k, sin_k = jnp.where(turned, cos[...], 1.0), jnp.where(turned, sin[...], 0.0)
    qkv[:, :128] = (raw[:, :128] * cos[...] + raw[:, 256:384] * sin[...]).astype(bf16)
    qkv[:, 128:] = (raw[:, 128:256] * cos_k + raw[:, 384:] * sin_k).astype(bf16)
    for i in range(LENGTH // QB):
        part, count = slice(i * QB, (i + 1) * QB), (i + 1) * QB
        keys, values = qkv[:count, 128:192], qkv[:count, 192:256]
        for h in range(2):
            scores = masked_scores(
                qkv[part, h * 64 : (h + 1) * 64], keys, seg_col[part], seg_row[:, :count], i * QB
            )
            top = jnp.max(scores, axis=-1, keepdims=True)
            expo = jnp.exp(scores - top)
            total = jnp.sum(expo, axis=-1, keepdims=True)
            probs = (expo * (1.0 / total)).astype(bf16)
            attended[part, h * 64 : (h + 1) * 64] = dot(probs, values).astype(bf16)
            lse[part, h : h + 1] = top + jnp.log(total)


def attend(x_all, gain, w, cos, sin, seg_col, seg_row):
    return pl.pallas_call(
        attend_kernel,
        out_shape=[
            jax.ShapeDtypeStruct((LENGTH, D), bf16),
            jax.ShapeDtypeStruct((LENGTH, 256), bf16),
            jax.ShapeDtypeStruct((LENGTH, 128), bf16),
            jax.ShapeDtypeStruct((LENGTH, 2), f32),
        ],
        compiler_params=pltpu.CompilerParams(vmem_limit_bytes=56 * 2**20),
        cost_estimate=pl.CostEstimate(
            flops=3 * 10**9, bytes_accessed=6 * 2**20, transcendentals=2 * 10**6
        ),
        name="attend",
    )(x_all, gain, w, cos, sin, seg_col, seg_row)


def half_swap(v):
    lane = lax.broadcasted_iota(jnp.int32, v.shape, 1)
    return jnp.where(lane % 64 < 32, -pltpu.roll(v, 96, 1), pltpu.roll(v, 32, 1))


def attend_back_kernel(
    x,
    normed,
    w,
    qkv,
    lse,
    dbranch,
    w_out,
    attended,
    extra,
    cos,
    sin,
    seg_col,
    seg_row,
    payload,
    dnormed,
    dout,
    dq,
    dkv,
):
    dout[...] = dot(dbranch[...], w_out[...], NT).astype(bf16)
    payload[:, 3072:] = dot(attended[...], dbranch[...], TN).astype(bf16)
    dkv[...] = jnp.zeros_like(dkv)
    scale = HEAD_DIM**-0.5
    for i in range(LENGTH // QB):
        part, count = slice(i * QB, (i + 1) * QB), (i + 1) * QB
        keys, values = qkv[:count, 128:192], qkv[:count, 192:256]
        dk_part, dv_part = 0.0, 0.0
        for h in range(2):
            q_h, do_h = qkv[part, h * 64 : (h + 1) * 64], dout[part, h * 64 : (h + 1) * 64]
            scores = masked_scores(q_h, keys, seg_col[part], seg_row[:, :count], i * QB)
            probs = jnp.exp(scores - lse[part, h : h + 1])
            dprobs = dot(do_h, values, NT)
            delta = jnp.sum(probs * dprobs, axis=-1, keepdims=True)
            dscores = (probs * (dprobs - delta)).astype(bf16)
            dq[part, h * 64 : (h + 1) * 64] = dot(dscores, keys) * scale
            dk_part = dk_part + dot(dscores, q_h, TN)
            dv_part = dv_part + dot(probs.astype(bf16), do_h, TN)
        dkv[:count, :64] += dk_part * scale
        dkv[:count, 64:] += dv_part
    d_q, d_kv = dq[...], dkv[...]
    turned = lax.broadcasted_iota(jnp.int32, (1, 128), 1) < HEAD_DIM
    cos_k, sin_k = jnp.where(turned, cos[...], 1.0), jnp.where(turned, sin[...], 0.0)
    d_q = (d_q * cos[...] - half_swap(d_q) * sin[...]).astype(bf16)
    d_kv = (d_kv * cos_k - half_swap(d_kv) * sin_k).astype(bf16)
    dqkv = jnp.concatenate([d_q, d_kv], axis=1)
    small = dot(normed[...], dqkv, TN).astype(bf16)
    d_n = dot(dqkv, w[...], NT)
    dnormed[...] = d_n.astype(bf16)
    x_full = x[...].astype(f32)
    r = lax.rsqrt(jnp.mean(x_full * x_full, axis=-1, keepdims=True) + epsilon)
    dgain = jnp.sum(d_n * (x_full * r), axis=0, keepdims=True)
    lane = lax.broadcasted_iota(jnp.int32, (LP, 128), 1)
    for f in range(NF):
        part = slice(f * LP, (f + 1) * LP)
        payload[:, f * 384 : f * 384 + 256] = small[part]
        column = jnp.transpose(jnp.broadcast_to(dgain[:, part], (128, LP)))
        payload[:, f * 384 + 256 : (f + 1) * 384] = jnp.where(
            lane == EXPERTS + 1, column, extra[part].astype(f32)
        ).astype(bf16)


def attend_back(*operands):
    return pl.pallas_call(
        attend_back_kernel,
        out_shape=[
            jax.ShapeDtypeStruct((LP, 4096), bf16),
            jax.ShapeDtypeStruct((LENGTH, D), bf16),
        ],
        scratch_shapes=[
            pltpu.VMEM((LENGTH, 128), bf16),
            pltpu.VMEM((LENGTH, 128), f32),
            pltpu.VMEM((LENGTH, 128), f32),
        ],
        compiler_params=pltpu.CompilerParams(vmem_limit_bytes=56 * 2**20),
        cost_estimate=pl.CostEstimate(
            flops=6 * 10**9, bytes_accessed=14 * 2**20, transcendentals=2 * 10**6
        ),
        name="attend_back",
    )(*operands)


def local(
    layer_input,
    segment_ids,
    routes,
    attn_gain,
    w_query,
    w_key,
    w_value,
    w_output,
    w_router,
    ffn_gain,
    w_gate,
    w_up,
    w_down,
    cotangent,
):
    e = lax.axis_index("expert")
    x_own = layer_input[0]
    cot_own = cotangent[0]
    columns = jnp.concatenate(
        [
            w_query.reshape(LP, NF, 128),
            w_key.reshape(LP, NF, 64),
            w_value.reshape(LP, NF, 64),
        ],
        axis=-1,
    ).swapaxes(0, 1)
    extra = jnp.concatenate(
        [
            jnp.concatenate([attn_gain, ffn_gain])[None],
            w_router.reshape(16, 256),
            jnp.zeros((15, 256), bf16),
        ],
        axis=0,
    )
    payload = jnp.concatenate([columns, jnp.broadcast_to(extra[None], (NF, 32, 256))], axis=1)
    x_all, got = gather_fsdp(x_own, swap_fsdp(payload))
    x_all = x_all.reshape(LENGTH, D)
    w_qkv = got[:, :LP].reshape(D, 256)
    gain_one = got[:, LP, :128].reshape(D).astype(f32)
    gain_two = got[:, LP, 128:].reshape(D).astype(f32)
    router = got[:, LP + 1 : LP + 17].reshape(D, EXPERTS)
    w_own = jnp.concatenate(
        [w_gate[0], w_up[0], w_gate[1], w_up[1], w_down[0].T, w_down[1].T], axis=1
    )
    w_exp = lax.all_gather(w_own, "fsdp", axis=0, tiled=True)
    cot_all = lax.all_gather(
        jnp.concatenate(
            [cot_own, routes[0].astype(bf16).reshape(1, D), jnp.zeros((7, D), bf16)], axis=0
        ),
        "expert",
        axis=0,
    )

    heads_w = w_qkv[:, :192].reshape(D, 3, 2, HEAD_DIM // 2)
    swapped = jnp.stack([-heads_w[:, :, 1], heads_w[:, :, 0]], axis=2).reshape(D, 192)
    w_both = jnp.concatenate([w_qkv, swapped, jnp.zeros((D, 64), bf16)], axis=1)
    cos_wide, sin_wide = (jnp.asarray(table) for table in rope_tables())
    seg_row = segment_ids
    seg_col = segment_ids.reshape(LENGTH, 1)
    normed, qkv, attended, lse = attend(
        x_all, gain_one[None], w_both, cos_wide, sin_wide, seg_col, seg_row
    )
    w_out, attended = gather_fsdp(after(w_output, x_all), attended)
    w_out = w_out.reshape(D, D)
    routes_all = cot_all[:, LP].reshape(NE, LP, 8).astype(jnp.int32)

    own_ids = 2 * e + jnp.arange(2, dtype=jnp.int32)
    chosen_own = jnp.any(routes_all[:, :, :, None] == own_ids, axis=2)
    before = (jnp.arange(LP)[:, None] > jnp.arange(LP)[None, :]).astype(bf16)
    rank = jnp.einsum(
        "ts,bsj->bjt", before, chosen_own.astype(bf16), preferred_element_type=f32
    )
    slot_ids = jnp.arange(SLOTS, dtype=f32)
    member_t = chosen_own.swapaxes(1, 2)
    pick = (
        ((rank[:, :, None, :] == slot_ids[:, None]) & member_t[:, :, None, :])
        .astype(bf16)
        .reshape(NE, 2 * SLOTS, LP)
    )
    pick_t = pick.swapaxes(1, 2)
    member_all = jnp.any(
        routes_all[:, :, :, None] == jnp.arange(128, dtype=jnp.int32), axis=2
    ).astype(bf16)
    member_own = jnp.any(
        routes[0][:, :, None] == jnp.arange(EXPERTS, dtype=jnp.int32), axis=1
    )
    router_wide = jnp.concatenate([router, jnp.zeros((D, 128 - EXPERTS), bf16)], axis=1)

    attended_own = swap_fsdp(attended.reshape(NF, LP, 128)).swapaxes(0, 1).reshape(LP, D)
    after_attn = x_own.astype(f32) + jnp.dot(attended_own, w_out, preferred_element_type=f32)
    r_two = lax.rsqrt(jnp.mean(after_attn * after_attn, axis=-1, keepdims=True) + epsilon)
    normed_two = (after_attn * r_two * gain_two).astype(bf16)

    rows_all, (pick, pick_t, member_all) = gather_expert(
        normed_two, (pick, pick_t, member_all)
    )
    inputs, hidden, dboth, dres, mix_part, drows_part = experts(
        e[None], rows_all, cot_all, member_all, pick, pick_t, router_wide, w_exp
    )
    grad_exp = expert_weights(inputs, dres, dboth, hidden)
    drows, grad_exp = scatter_expert(drows_part, grad_exp)
    grad_exp = lax.psum_scatter(grad_exp, "fsdp", scatter_dimension=0)

    logits = jnp.dot(normed_two, router, preferred_element_type=f32)
    gates = masked_gates(logits, member_own)
    dgate_own = drows[:, D : D + EXPERTS] + drows[:, D + EXPERTS : D + 2 * EXPERTS]
    dlogits = gates * (dgate_own - jnp.sum(gates * dgate_own, axis=-1, keepdims=True))
    dnormed_two = drows[:, :D] + jnp.einsum(
        "te,de->td", dlogits, router.astype(f32), precision=highest
    )
    dafter_norm, part_gain_two = norm_back(dnormed_two, after_attn, gain_two)
    dafter = cot_own.astype(f32) + dafter_norm
    dbranch = dafter.astype(bf16)
    dbranch_all = gather_fsdp(dbranch)[0].reshape(LENGTH, D)
    part_router = jnp.einsum(
        "td,te->de", normed_two.astype(f32), dlogits, precision=highest
    )

    extra = jnp.concatenate(
        [
            part_router.astype(bf16),
            part_gain_two[:, None].astype(bf16),
            jnp.zeros((D, 128 - EXPERTS - 1), bf16),
        ],
        axis=-1,
    )

    payload, dnormed_part = attend_back(
        x_all,
        normed,
        w_qkv,
        qkv,
        lse,
        dbranch_all,
        w_output,
        attended,
        extra,
        cos_wide,
        sin_wide,
        seg_col,
        seg_row,
    )
    mix, (payload, dnormed_part, grad_exp) = scatter_expert(
        after(mix_part, dbranch), (payload, dnormed_part, grad_exp)
    )
    dnormed = lax.psum_scatter(
        dnormed_part.reshape(NF, LP, D), "fsdp", scatter_dimension=0
    ).astype(f32)
    dinput_norm, _ = norm_back(dnormed, x_own.astype(f32), gain_one)
    grad_input = (dafter + dinput_norm).astype(bf16)

    grad_exp = grad_exp.astype(f32)
    grad_gate = jnp.stack([grad_exp[:, :512], grad_exp[:, 1024:1536]])
    grad_up = jnp.stack([grad_exp[:, 512:1024], grad_exp[:, 1536:2048]])
    grad_down = jnp.stack([grad_exp[:, 2048:2560].T, grad_exp[:, 2560:].T])

    payload = lax.all_to_all(
        payload.reshape(NE, LP // NE, 4096), "expert", split_axis=0, concat_axis=0, tiled=True
    )
    payload = jnp.sum(payload.astype(f32), axis=0).astype(bf16)
    small = swap_fsdp(payload[:, :3072].reshape(LP // NE, NF, 384).swapaxes(0, 1))
    chunk = jnp.concatenate(
        [
            small[:, :, :256].swapaxes(0, 1).reshape(LP // NE, 2048),
            jnp.sum(small[:, :, 256:].astype(f32), axis=0).astype(bf16),
            payload[:, 3072:],
        ],
        axis=-1,
    )
    chunk, mix = lax.optimization_barrier((chunk, mix))
    layer_output = (after_attn + mix).astype(bf16)
    total_sum = lax.all_to_all(
        jnp.broadcast_to(chunk[None], (NE,) + chunk.shape),
        "expert",
        split_axis=0,
        concat_axis=0,
        tiled=True,
    ).reshape(LP, 3200)
    total_sum = total_sum.astype(f32)
    heads_sum = total_sum[:, :2048].reshape(LP, NF, 256)
    grad_output = total_sum[:, 2176:]
    grad_query = heads_sum[:, :, :128].reshape(LP, 1024)
    grad_key = heads_sum[:, :, 128:192].reshape(LP, 512)
    grad_value = heads_sum[:, :, 192:].reshape(LP, 512)
    grad_router = total_sum[:, 2048:2080]
    grad_gain_two = total_sum[:, 2080]
    grad_gain_one = total_sum[:, 2081]
    return (
        layer_output[None],
        grad_input[None],
        grad_gain_one,
        grad_query,
        grad_key,
        grad_value,
        grad_output,
        grad_router,
        grad_gain_two,
        grad_gate,
        grad_up,
        grad_down,
    )


def solution(mesh):
    placed = (
        P("expert", "fsdp", None),
        P("expert", None),
        P("expert", "fsdp", None),
        P("fsdp"),
        P("fsdp", None),
        P("fsdp", None),
        P("fsdp", None),
        P("fsdp", None),
        P("fsdp", None),
        P("fsdp"),
        P("expert", "fsdp", None),
        P("expert", "fsdp", None),
        P("expert", None, "fsdp"),
        P("expert", "fsdp", None),
    )
    return jax.shard_map(
        local,
        mesh=mesh,
        in_specs=placed,
        out_specs=(
            P("expert", "fsdp", None),
            P("expert", "fsdp", None),
            P("fsdp"),
            P("fsdp", None),
            P("fsdp", None),
            P("fsdp", None),
            P("fsdp", None),
            P("fsdp", None),
            P("fsdp"),
            P("expert", "fsdp", None),
            P("expert", "fsdp", None),
            P("expert", None, "fsdp"),
        ),
        check_vma=False,
    )
```

```python
import jax
import jax.numpy as jnp
import numpy as np
from jax import lax
from jax.experimental import pallas as pl
from jax.experimental.pallas import tpu as pltpu
from jax.sharding import PartitionSpec as P

HEAD_DIM = 64
EXPERTS = 32
SLOTS = 64
NF = 8
NE = 16
LP = 128
LENGTH = 1024
D = 1024
FF = 512

epsilon = 1e-06
rope_base = 10000.0
highest = lax.Precision.HIGHEST
bf16 = jnp.bfloat16
f32 = jnp.float32


def shift_x(v, k):
    return lax.ppermute(v, "fsdp", [(i, (i + 2 * k) % NF) for i in range(NF)])


def swap_core(v):
    return lax.ppermute(v, "fsdp", [(i, i ^ 1) for i in range(NF)])


def shift_z(v, k):
    return lax.ppermute(v, "expert", [(i, (i // 4) * 4 + (i + k) % 4) for i in range(NE)])


def shift_y(v, k):
    return lax.ppermute(v, "expert", [(i, (i + 4 * k) % NE) for i in range(NE)])


def put(buffer, piece, place):
    return lax.dynamic_update_index_in_dim(buffer, piece, place, 0)


def ring_gather(shift, v, place):
    got = [(v, place)] + [(shift(v, k), (place - k) % 4) for k in (1, 3, 2)]
    out = jnp.zeros((4,) + v.shape, v.dtype)
    for piece, where in got:
        out = put(out, piece, where)
    return out


def ring_gather_halves(shift, v, place):
    left, right = shift(v, 1), shift(v, 3)
    n = v.shape[0] // 2
    far = (shift(left[:n], 1), shift(right[n:], 3))
    out = jnp.zeros((4,) + v.shape, v.dtype)
    for piece, where in ((v, place), (left, (place - 1) % 4), (right, (place + 1) % 4)):
        out = put(out, piece, where)
    return put(out, jnp.concatenate(far, axis=0), (place + 2) % 4)


def gather_fsdp(v, beside=None):
    mine = ring_gather(shift_x, v, lax.axis_index("fsdp") // 2)
    if beside is not None:
        mine, beside = lax.optimization_barrier((mine, beside))
    return mine, swap_core(mine), beside


def in_order(mine, other):
    even = lax.axis_index("fsdp") % 2 == 0
    first = jnp.where(even, mine, other)
    second = jnp.where(even, other, mine)
    return jnp.stack([first, second], axis=1).reshape((NF * mine.shape[1],) + mine.shape[2:])


def gather_expert(v):
    e = lax.axis_index("expert")
    y, z = e // 4, e % 4
    n = v.shape[0] // 2
    a = ring_gather(shift_z, v[:n], z)
    b = ring_gather(shift_y, v[n:], y)
    return ring_gather_halves(shift_y, a, y), ring_gather_halves(shift_z, b, z)


def pieces_of(p, place):
    return [
        lax.dynamic_index_in_dim(p, (place + k) % 4, 0, keepdims=False) for k in range(4)
    ]


def ring_sum(shift, p, place):
    own, *others = pieces_of(p, place)
    total = own.astype(f32)
    for k in (1, 3, 2):
        total = total + shift(others[k - 1], k).astype(f32)
    return total


def ring_sum_halves(shift, p, place):
    own, right, far, left = pieces_of(p, place)
    n = own.shape[0] // 2
    from_left, from_right = shift(far[:n], 1), shift(far[n:], 3)
    right = jnp.concatenate([right[:n].astype(f32) + from_left.astype(f32), right[n:]], axis=0)
    left = jnp.concatenate([left[:n], left[n:].astype(f32) + from_right.astype(f32)], axis=0)
    total = own.astype(f32) + shift(right.astype(bf16), 1).astype(f32)
    return total + shift(left.astype(bf16), 3).astype(f32)


def scatter_expert(a, b, beside):
    e = lax.axis_index("expert")
    y, z = e // 4, e % 4
    a = ring_sum_halves(shift_y, a, y).astype(bf16)
    b = ring_sum_halves(shift_z, b, z).astype(bf16)
    a, b, beside = lax.optimization_barrier((a, b, beside))
    a = ring_sum(shift_z, a, z)
    b = ring_sum(shift_y, b, y)
    return jnp.concatenate([a, b], axis=0), beside


def scatter_fsdp(p):
    f = lax.axis_index("fsdp")
    x, c = f // 2, f % 2
    p = p.reshape((4, 2) + p.shape[1:])
    kept = lax.dynamic_index_in_dim(p, c, 1, keepdims=False)
    given = lax.dynamic_index_in_dim(p, 1 - c, 1, keepdims=False)
    pair = (kept.astype(f32) + swap_core(given).astype(f32)).astype(bf16)
    return ring_sum(shift_x, pair, x)


def after(v, first):
    return lax.optimization_barrier((v, first))[0]


def dot(a, b, dims=((1,), (0,))):
    return lax.dot_general(a, b, (dims, ((), ())), preferred_element_type=f32)


NT = ((1,), (1,))
TN = ((0,), (0,))


HALF = LP // 2


def expert_kernel(
    e_ref, rows_a, rows_b, cot, router, w, inputs, hidden, dboth, dres, mix, drows_a, drows_b
):
    e = e_ref[0]
    lane = lax.broadcasted_iota(jnp.int32, (1, 128), 1)
    ids = lax.broadcasted_iota(jnp.int32, (EXPERTS, LP), 0)
    ids_f = ids.astype(f32)
    slot_ids = lax.broadcasted_iota(jnp.int32, (SLOTS, LP), 0).astype(f32)
    earlier = (
        lax.broadcasted_iota(jnp.int32, (LP, LP), 0) < lax.broadcasted_iota(jnp.int32, (LP, LP), 1)
    ).astype(bf16)
    picks, gates, x_slots, c_slots = [], [], [], []
    for b in range(4):
        rows = jnp.concatenate([rows_a[0, b], rows_b[b, 0]], axis=0)
        routes = cot[b, LP:, :LP].astype(f32)
        has = routes[0:1] == ids_f
        for k in range(1, 8):
            has = has | (routes[k : k + 1] == ids_f)
        low = jnp.where(has, dot(router[...], rows, NT), -1e30)
        top = jnp.max(low, axis=0, keepdims=True)
        expo = jnp.where(has, jnp.exp(low - top), 0.0)
        soft = expo / jnp.sum(expo, axis=0, keepdims=True)
        pick_j, gate_j = [], []
        for j in range(2):
            here = ids == 2 * e + j
            member = jnp.sum(jnp.where(here & has, 1.0, 0.0), axis=0, keepdims=True)
            gate = jnp.sum(jnp.where(here, soft, 0.0), axis=0, keepdims=True)
            wide = jnp.broadcast_to(member, (16, LP)).astype(bf16)
            rank = dot(wide, earlier)[0:1]
            pick = jnp.where((rank == slot_ids) & (member > 0.5), 1.0, 0.0)
            pick_j.append(pick.astype(bf16))
            gate_j.append(jnp.sum(pick * gate, axis=1, keepdims=True))
        pick = jnp.concatenate(pick_j, axis=0)
        picks.append(pick)
        gates.append(gate_j)
        x_slots.append(dot(pick, rows).astype(bf16))
        c_slots.append(dot(pick, cot[b, :LP]))
    weighted, dassign, extra = [], [], []
    for j in range(2):
        part = slice(j * SLOTS, (j + 1) * SLOTS)
        x_in = jnp.concatenate([v[part] for v in x_slots], axis=0)
        c_in = jnp.concatenate([v[part] for v in c_slots], axis=0)
        gate_in = jnp.concatenate([v[j] for v in gates], axis=0)
        w_g = w[:, j * 1024 : j * 1024 + FF]
        w_u = w[:, j * 1024 + FF : (j + 1) * 1024]
        w_d = w[:, 2048 + j * FF : 2048 + (j + 1) * FF]
        gate_val = dot(x_in, w_g)
        up_val = dot(x_in, w_u)
        sig = 1.0 / (1.0 + jnp.exp(-gate_val))
        activated = gate_val * sig
        hid = (activated * up_val).astype(bf16)
        result = dot(hid, w_d, NT).astype(bf16).astype(f32)
        dgate = jnp.sum(result * c_in, axis=-1, keepdims=True)
        dresult = (gate_in * c_in).astype(bf16)
        dhidden = dot(dresult, w_d)
        dgate_val = (dhidden * up_val * sig * (1.0 + gate_val * (1.0 - sig))).astype(bf16)
        dup_val = (dhidden * activated).astype(bf16)
        da = (dot(dgate_val, w_g, NT) + dot(dup_val, w_u, NT)).astype(bf16)
        weighted.append((gate_in * result).astype(bf16))
        dassign.append(da)
        dg_high = dgate.astype(bf16).astype(f32)
        dg_low = dgate - dg_high
        extra.append(
            (
                jnp.where(lane == 2 * e + j, dg_high, 0.0)
                + jnp.where(lane == EXPERTS + 2 * e + j, dg_low, 0.0)
            ).astype(bf16)
        )
        inputs[j] = x_in
        hidden[j] = hid
        dboth[j, :, :FF] = dgate_val
        dboth[j, :, FF:] = dup_val
        dres[j] = dresult
    for b in range(4):
        part = slice(b * SLOTS, (b + 1) * SLOTS)
        weighted_b = jnp.concatenate([weighted[0][part], weighted[1][part]], axis=0)
        dassign_b = jnp.concatenate([dassign[0][part], dassign[1][part]], axis=0)
        extra_b = jnp.concatenate([extra[0][part], extra[1][part]], axis=0)
        mix[b] = dot(picks[b], weighted_b, TN).astype(bf16)
        d_rows = dot(picks[b], dassign_b, TN).astype(bf16)
        d_extra = dot(picks[b], extra_b, TN).astype(bf16)
        drows_a[0, b, :, :D] = d_rows[:HALF]
        drows_a[0, b, :, D:] = d_extra[:HALF]
        drows_b[b, 0, :, :D] = d_rows[HALF:]
        drows_b[b, 0, :, D:] = d_extra[HALF:]


def experts(e, rows_a, rows_b, cot_all, router, w):
    rows = NE * SLOTS
    step = rows // 4
    return pl.pallas_call(
        expert_kernel,
        grid=(4,),
        in_specs=[
            pl.BlockSpec(memory_space=pltpu.SMEM),
            pl.BlockSpec((1, 4, HALF, D), lambda i: (i, 0, 0, 0)),
            pl.BlockSpec((4, 1, HALF, D), lambda i: (0, i, 0, 0)),
            pl.BlockSpec((4, LP + 16, D), lambda i: (i, 0, 0)),
            pl.BlockSpec((EXPERTS, D), lambda i: (0, 0)),
            pl.BlockSpec((D, 3072), lambda i: (0, 0), pipeline_mode=pl.Buffered(1)),
        ],
        out_specs=[
            pl.BlockSpec((2, step, D), lambda i: (0, i, 0)),
            pl.BlockSpec((2, step, FF), lambda i: (0, i, 0)),
            pl.BlockSpec((2, step, 2 * FF), lambda i: (0, i, 0)),
            pl.BlockSpec((2, step, D), lambda i: (0, i, 0)),
            pl.BlockSpec((4, LP, D), lambda i: (i, 0, 0)),
            pl.BlockSpec((1, 4, HALF, D + 128), lambda i: (i, 0, 0, 0)),
            pl.BlockSpec((4, 1, HALF, D + 128), lambda i: (0, i, 0, 0)),
        ],
        out_shape=[
            jax.ShapeDtypeStruct((2, rows, D), bf16),
            jax.ShapeDtypeStruct((2, rows, FF), bf16),
            jax.ShapeDtypeStruct((2, rows, 2 * FF), bf16),
            jax.ShapeDtypeStruct((2, rows, D), bf16),
            jax.ShapeDtypeStruct((NE, LP, D), bf16),
            jax.ShapeDtypeStruct((4, 4, HALF, D + 128), bf16),
            jax.ShapeDtypeStruct((4, 4, HALF, D + 128), bf16),
        ],
        compiler_params=pltpu.CompilerParams(vmem_limit_bytes=56 * 2**20),
        cost_estimate=pl.CostEstimate(
            flops=14 * 10**9, bytes_accessed=30 * 2**20, transcendentals=10**6
        ),
        name="experts",
    )(e, rows_a, rows_b, cot_all, router, w)


def weight_kernel(inputs, dres, dboth, hidden, out):
    for j in range(2):
        out[:, :, j * 1024 : (j + 1) * 1024] = (
            dot(inputs[j], dboth[j], TN).astype(bf16).reshape(2, LP, 1024)
        )
        out[:, :, 2048 + j * FF : 2048 + (j + 1) * FF] = (
            dot(dres[j], hidden[j], TN).astype(bf16).reshape(2, LP, FF)
        )


def expert_weights(inputs, dres, dboth, hidden):
    rows = NE * SLOTS
    return pl.pallas_call(
        weight_kernel,
        grid=(4,),
        in_specs=[
            pl.BlockSpec((2, rows, 256), lambda i: (0, 0, i)),
            pl.BlockSpec((2, rows, 256), lambda i: (0, 0, i)),
            pl.BlockSpec((2, rows, 2 * FF), lambda i: (0, 0, 0)),
            pl.BlockSpec((2, rows, FF), lambda i: (0, 0, 0)),
        ],
        out_specs=pl.BlockSpec((2, LP, 3072), lambda i: (i, 0, 0)),
        out_shape=jax.ShapeDtypeStruct((NF, LP, 3072), bf16),
        compiler_params=pltpu.CompilerParams(vmem_limit_bytes=56 * 2**20),
        cost_estimate=pl.CostEstimate(
            flops=7 * 10**9, bytes_accessed=20 * 2**20, transcendentals=0
        ),
        name="expert_weights",
    )(inputs, dres, dboth, hidden)


def swap_fsdp(v):
    return lax.all_to_all(v, "fsdp", split_axis=0, concat_axis=0, tiled=True)


def rope_tables():
    exponent = np.arange(HEAD_DIM // 2, dtype=np.float32) * np.float32(2.0 / HEAD_DIM)
    inverse = np.power(np.float32(rope_base), -exponent).astype(np.float32)
    angles = np.arange(LENGTH, dtype=np.float32)[:, None] * inverse[None, :]
    wide = np.tile(angles.astype(np.float32), (1, 4))
    return np.cos(wide).astype(np.float32), np.sin(wide).astype(np.float32)


def masked_gates(logits, member):
    low = jnp.where(member, logits, -1e30)
    top = jnp.max(low, axis=-1, keepdims=True)
    expo = jnp.where(member, jnp.exp(low - top), 0.0)
    return expo / jnp.sum(expo, axis=-1, keepdims=True)


def norm_back(u, v, gain):
    r = lax.rsqrt(jnp.mean(v * v, axis=-1, keepdims=True) + epsilon)
    inner = jnp.mean(gain * u * v, axis=-1, keepdims=True)
    return r * gain * u - v * (r * r * r) * inner, jnp.sum(u * v * r, axis=0)


def masked_scores(q_h, keys, seg_col, seg_row, first):
    rows, count = q_h.shape[0], keys.shape[0]
    scores = dot(q_h, keys, NT) * HEAD_DIM**-0.5
    row = lax.broadcasted_iota(jnp.int32, (rows, count), 0) + first
    column = lax.broadcasted_iota(jnp.int32, (rows, count), 1)
    allowed = (seg_col == seg_row) & (column <= row)
    return jnp.where(allowed, scores, -1e30)


QB = 256


def order_rows(core, mine, other, out):
    for x in range(4):
        own = pl.multiple_of(x * 2 * LP + core * LP, LP)
        out[pl.ds(own, LP)] = mine[x]
        beside = pl.multiple_of(x * 2 * LP + (1 - core) * LP, LP)
        out[pl.ds(beside, LP)] = other[x]


def pack_kernel(w_query, w_key, w_value, w_router, gains, out):
    rest = jnp.concatenate(
        [w_router[...], gains[...], jnp.zeros((LP, 128 - EXPERTS - 2), bf16)], axis=1
    )
    for f in range(NF):
        out[f, :, :128] = w_query[:, f * 128 : (f + 1) * 128]
        out[f, :, 128:192] = w_key[:, f * 64 : (f + 1) * 64]
        out[f, :, 192:256] = w_value[:, f * 64 : (f + 1) * 64]
        out[f, :, 256:] = rest


def pack(*operands):
    return pl.pallas_call(
        pack_kernel,
        out_shape=jax.ShapeDtypeStruct((NF, LP, 384), bf16),
        cost_estimate=pl.CostEstimate(flops=10**6, bytes_accessed=2 * 2**20, transcendentals=0),
        name="pack",
    )(*operands)


def half_swap(v):
    lane = lax.broadcasted_iota(jnp.int32, v.shape, 1)
    return jnp.where(lane % 64 < 32, -pltpu.roll(v, 96, 1), pltpu.roll(v, 32, 1))


def attend_kernel(
    core,
    mine,
    other,
    got,
    cos,
    sin,
    seg_col,
    seg_row,
    x,
    normed,
    qkv,
    attended,
    attended_send,
    lse,
    rest,
):
    order_rows(core[0], mine, other, x)
    for f in range(NF):
        part = slice(f * LP, (f + 1) * LP)
        rest[:, part] = jnp.transpose(got[part, 256:].astype(f32))[: EXPERTS + 8]
    x_full = x[...].astype(f32)
    r = lax.rsqrt(jnp.mean(x_full * x_full, axis=-1, keepdims=True) + epsilon)
    normed[...] = (x_full * r * rest[EXPERTS : EXPERTS + 1]).astype(bf16)
    raw = dot(normed[...], got[:, :256])
    turned = lax.broadcasted_iota(jnp.int32, (1, 128), 1) < HEAD_DIM
    cos_k, sin_k = jnp.where(turned, cos[...], 1.0), jnp.where(turned, sin[...], 0.0)
    raw_q, raw_kv = raw[:, :128], raw[:, 128:]
    qkv[:, :128] = (raw_q * cos[...] + half_swap(raw_q) * sin[...]).astype(bf16)
    qkv[:, 128:] = (raw_kv * cos_k + half_swap(raw_kv) * sin_k).astype(bf16)
    for i in range(LENGTH // QB):
        part, count = slice(i * QB, (i + 1) * QB), (i + 1) * QB
        keys, values = qkv[:count, 128:192], qkv[:count, 192:256]
        for h in range(2):
            scores = masked_scores(
                qkv[part, h * 64 : (h + 1) * 64], keys, seg_col[part], seg_row[:, :count], i * QB
            )
            top = jnp.max(scores, axis=-1, keepdims=True)
            expo = jnp.exp(scores - top)
            total = jnp.sum(expo, axis=-1, keepdims=True)
            probs = (expo * (1.0 / total)).astype(bf16)
            attended[part, h * 64 : (h + 1) * 64] = dot(probs, values).astype(bf16)
            lse[part, h : h + 1] = top + jnp.log(total)
        attended_send[2 * i : 2 * i + 2] = attended[part].reshape(2, LP, 128)


VMEM = pl.BlockSpec(memory_space=pltpu.VMEM)
SMEM = pl.BlockSpec(memory_space=pltpu.SMEM)


def attend(*operands):
    return pl.pallas_call(
        attend_kernel,
        in_specs=[SMEM] + [VMEM] * (len(operands) - 1),
        out_shape=[
            jax.ShapeDtypeStruct((LENGTH, D), bf16),
            jax.ShapeDtypeStruct((LENGTH, D), bf16),
            jax.ShapeDtypeStruct((LENGTH, 256), bf16),
            jax.ShapeDtypeStruct((LENGTH, 128), bf16),
            jax.ShapeDtypeStruct((NF, LP, 128), bf16),
            jax.ShapeDtypeStruct((LENGTH, 2), f32),
            jax.ShapeDtypeStruct((EXPERTS + 8, D), f32),
        ],
        compiler_params=pltpu.CompilerParams(vmem_limit_bytes=56 * 2**20),
        cost_estimate=pl.CostEstimate(
            flops=3 * 10**9, bytes_accessed=6 * 2**20, transcendentals=2 * 10**6
        ),
        name="attend",
    )(*operands)


def branch_back_kernel(core, mine, other, w_out, attended, part_output, dout, dbranch):
    order_rows(core[0], mine, other, dbranch)
    part_output[...] = dot(attended[...], dbranch[...], TN).astype(bf16)
    dout[...] = dot(dbranch[...], w_out[...], NT).astype(bf16)


def branch_back(*operands):
    return pl.pallas_call(
        branch_back_kernel,
        in_specs=[SMEM] + [VMEM] * (len(operands) - 1),
        out_shape=[
            jax.ShapeDtypeStruct((LP, D), bf16),
            jax.ShapeDtypeStruct((LENGTH, 128), bf16),
        ],
        scratch_shapes=[pltpu.VMEM((LENGTH, D), bf16)],
        compiler_params=pltpu.CompilerParams(vmem_limit_bytes=56 * 2**20),
        cost_estimate=pl.CostEstimate(
            flops=6 * 10**8, bytes_accessed=5 * 2**20, transcendentals=0
        ),
        name="branch_back",
    )(*operands)


def attend_back_kernel(
    x, normed, got, qkv, lse, dout, extra, cos, sin, seg_col, seg_row, payload, dnormed, dq, dkv
):
    dkv[...] = jnp.zeros_like(dkv)
    scale = HEAD_DIM**-0.5
    for i in range(LENGTH // QB):
        part, count = slice(i * QB, (i + 1) * QB), (i + 1) * QB
        keys, values = qkv[:count, 128:192], qkv[:count, 192:256]
        dk_part, dv_part = 0.0, 0.0
        for h in range(2):
            q_h, do_h = qkv[part, h * 64 : (h + 1) * 64], dout[part, h * 64 : (h + 1) * 64]
            scores = masked_scores(q_h, keys, seg_col[part], seg_row[:, :count], i * QB)
            probs = jnp.exp(scores - lse[part, h : h + 1])
            dprobs = dot(do_h, values, NT)
            delta = jnp.sum(probs * dprobs, axis=-1, keepdims=True)
            dscores = (probs * (dprobs - delta)).astype(bf16)
            dq[part, h * 64 : (h + 1) * 64] = dot(dscores, keys) * scale
            dk_part = dk_part + dot(dscores, q_h, TN)
            dv_part = dv_part + dot(probs.astype(bf16), do_h, TN)
        dkv[:count, :64] += dk_part * scale
        dkv[:count, 64:] += dv_part
    d_q, d_kv = dq[...], dkv[...]
    turned = lax.broadcasted_iota(jnp.int32, (1, 128), 1) < HEAD_DIM
    cos_k, sin_k = jnp.where(turned, cos[...], 1.0), jnp.where(turned, sin[...], 0.0)
    d_q = (d_q * cos[...] - half_swap(d_q) * sin[...]).astype(bf16)
    d_kv = (d_kv * cos_k - half_swap(d_kv) * sin_k).astype(bf16)
    dqkv = jnp.concatenate([d_q, d_kv], axis=1)
    payload[:, :256] = dot(normed[...], dqkv, TN).astype(bf16)
    d_n = dot(dqkv, got[:, :256], NT)
    dnormed[...] = d_n.astype(bf16).reshape(NF, LP, D)
    x_full = x[...].astype(f32)
    r = lax.rsqrt(jnp.mean(x_full * x_full, axis=-1, keepdims=True) + epsilon)
    dgain = jnp.sum(d_n * (x_full * r), axis=0, keepdims=True)
    lane = lax.broadcasted_iota(jnp.int32, (LP, 128), 1)
    for f in range(NF):
        part = slice(f * LP, (f + 1) * LP)
        column = jnp.transpose(jnp.broadcast_to(dgain[:, part], (128, LP)))
        payload[part, 256:] = jnp.where(
            lane == EXPERTS + 1, column, extra[part].astype(f32)
        ).astype(bf16)


def attend_back(*operands):
    return pl.pallas_call(
        attend_back_kernel,
        out_shape=[
            jax.ShapeDtypeStruct((LENGTH, 384), bf16),
            jax.ShapeDtypeStruct((NF, LP, D), bf16),
        ],
        scratch_shapes=[
            pltpu.VMEM((LENGTH, 128), f32),
            pltpu.VMEM((LENGTH, 128), f32),
        ],
        compiler_params=pltpu.CompilerParams(vmem_limit_bytes=56 * 2**20),
        cost_estimate=pl.CostEstimate(
            flops=6 * 10**9, bytes_accessed=14 * 2**20, transcendentals=2 * 10**6
        ),
        name="attend_back",
    )(*operands)


def unpack_kernel(total, query, key, value, output, router, rest_t):
    query[...] = total[:, :1024].astype(f32)
    key[...] = total[:, 1024:1536].astype(f32)
    value[...] = total[:, 1536:2048].astype(f32)
    output[...] = total[:, 2176:].astype(f32)
    rest = total[:, 2048:2176].astype(f32)
    router[...] = rest[:, :EXPERTS]
    rest_t[...] = jnp.transpose(rest)


def unpack(total):
    return pl.pallas_call(
        unpack_kernel,
        out_shape=[
            jax.ShapeDtypeStruct((LP, columns), f32) for columns in (D, FF, FF, D, EXPERTS, 128)
        ],
        cost_estimate=pl.CostEstimate(flops=10**6, bytes_accessed=3 * 2**20, transcendentals=0),
        name="unpack",
    )(total)


def unpack_experts_kernel(grads, gate, up, down):
    for j in range(2):
        gate[j] = grads[:, j * 1024 : j * 1024 + FF].astype(f32)
        up[j] = grads[:, j * 1024 + FF : (j + 1) * 1024].astype(f32)
        down[j] = jnp.transpose(grads[:, 2048 + j * FF : 2048 + (j + 1) * FF].astype(f32))


def unpack_experts(grads):
    return pl.pallas_call(
        unpack_experts_kernel,
        out_shape=[
            jax.ShapeDtypeStruct((2, LP, FF), f32),
            jax.ShapeDtypeStruct((2, LP, FF), f32),
            jax.ShapeDtypeStruct((2, FF, LP), f32),
        ],
        cost_estimate=pl.CostEstimate(flops=10**6, bytes_accessed=3 * 2**20, transcendentals=0),
        name="unpack_experts",
    )(grads)


HEAD_PARTS = (slice(0, 128), slice(128, 192), slice(192, 256))


def local(
    layer_input,
    segment_ids,
    routes,
    attn_gain,
    w_query,
    w_key,
    w_value,
    w_output,
    w_router,
    ffn_gain,
    w_gate,
    w_up,
    w_down,
    cotangent,
):
    e = lax.axis_index("expert")
    x_own = layer_input[0]
    cot_own = cotangent[0]
    payload = pack(
        w_query, w_key, w_value, w_router, jnp.stack([attn_gain, ffn_gain], axis=1)
    )
    core = (lax.axis_index("fsdp") % 2)[None]
    x_mine, x_other, got = gather_fsdp(x_own, swap_fsdp(payload))
    got = got.reshape(D, 384)
    cot_all = lax.all_gather(
        jnp.concatenate(
            [
                cot_own,
                jnp.pad(routes[0].astype(bf16).T, ((0, 8), (0, D - LP))),
            ],
            axis=0,
        ),
        "expert",
        axis=0,
    )

    cos_wide, sin_wide = (jnp.asarray(table) for table in rope_tables())
    seg_row = segment_ids
    seg_col = segment_ids.reshape(LENGTH, 1)
    x_all, normed, qkv, attended, attended_send, lse, rest = attend(
        core, x_mine, x_other, got, cos_wide, sin_wide, seg_col, seg_row
    )
    router_t = rest[:EXPERTS].astype(bf16)
    gain_one, gain_two = rest[EXPERTS], rest[EXPERTS + 1]
    w_mine, w_other, attended_send = gather_fsdp(after(w_output, x_other), attended_send)
    w_out = in_order(w_mine, w_other)
    member_own = jnp.any(
        routes[0][:, :, None] == jnp.arange(EXPERTS, dtype=jnp.int32), axis=1
    )

    attended_own = swap_fsdp(attended_send).swapaxes(0, 1).reshape(LP, D)
    w_own = jnp.concatenate(
        [w_gate[0], w_up[0], w_gate[1], w_up[1], w_down[0].T, w_down[1].T], axis=1
    )
    w_own = after(w_own, attended_own)
    w_exp = lax.all_gather(w_own, "fsdp", axis=0, tiled=True)
    after_attn = x_own.astype(f32) + jnp.dot(attended_own, w_out, preferred_element_type=f32)
    r_two = lax.rsqrt(jnp.mean(after_attn * after_attn, axis=-1, keepdims=True) + epsilon)
    normed_two = (after_attn * r_two * gain_two).astype(bf16)

    rows_a, rows_b = gather_expert(normed_two)
    inputs, hidden, dboth, dres, mix_part, drows_a, drows_b = experts(
        e[None], rows_a, rows_b, cot_all, router_t, w_exp
    )
    mix = lax.psum_scatter(mix_part, "expert", scatter_dimension=0)
    grad_exp = expert_weights(inputs, dres, dboth, hidden)
    drows, grad_exp = scatter_expert(drows_a, drows_b, grad_exp)
    grad_exp = lax.psum_scatter(grad_exp, "fsdp", scatter_dimension=0)

    logits = jnp.einsum("td,ed->te", normed_two, router_t, preferred_element_type=f32)
    gates = masked_gates(logits, member_own)
    dgate_own = drows[:, D : D + EXPERTS] + drows[:, D + EXPERTS : D + 2 * EXPERTS]
    dlogits = gates * (dgate_own - jnp.sum(gates * dgate_own, axis=-1, keepdims=True))
    dnormed_two = drows[:, :D] + jnp.einsum(
        "te,ed->td", dlogits, router_t.astype(f32), precision=highest
    )
    dafter_norm, part_gain_two = norm_back(dnormed_two, after_attn, gain_two)
    dafter = cot_own.astype(f32) + dafter_norm
    dbranch = dafter.astype(bf16)
    d_mine, d_other, _ = gather_fsdp(dbranch)
    part_router = jnp.einsum(
        "td,te->de", normed_two.astype(f32), dlogits, precision=highest
    )

    extra = jnp.concatenate(
        [
            part_router.astype(bf16),
            part_gain_two[:, None].astype(bf16),
            jnp.zeros((D, 128 - EXPERTS - 1), bf16),
        ],
        axis=-1,
    )

    part_output, dout = branch_back(core, d_mine, d_other, w_output, attended)
    part_output = lax.all_to_all(
        part_output.reshape(NE, LP // NE, D), "expert", split_axis=0, concat_axis=0, tiled=True
    )
    payload, dnormed_part = attend_back(
        x_all, normed, got, qkv, lse, dout, extra, cos_wide, sin_wide, seg_col, seg_row
    )
    payload, dnormed_part, mix, part_output = lax.optimization_barrier(
        (payload, dnormed_part, mix, part_output)
    )
    layer_output = (after_attn + mix.astype(f32)).astype(bf16)
    dnormed = scatter_fsdp(dnormed_part)
    dinput_norm, _ = norm_back(dnormed, x_own.astype(f32), gain_one)
    grad_input = (dafter + dinput_norm).astype(bf16)

    small = lax.all_to_all(
        payload.reshape(NF * NE, LP // NE, 384),
        ("fsdp", "expert"),
        split_axis=0,
        concat_axis=0,
        tiled=True,
    )
    small = jnp.sum(small.reshape(NF, NE, LP // NE, 384).astype(f32), axis=1)
    chunk_output = jnp.sum(part_output.astype(f32), axis=0)
    chunk = jnp.concatenate(
        [small[:, :, part].swapaxes(0, 1).reshape(LP // NE, -1) for part in HEAD_PARTS]
        + [jnp.sum(small[:, :, 256:], axis=0), chunk_output],
        axis=-1,
    ).astype(bf16)
    chunk, grad_exp = lax.optimization_barrier((chunk, grad_exp))
    grad_gate, grad_up, grad_down = unpack_experts(grad_exp)
    total_sum = lax.all_to_all(
        jnp.broadcast_to(chunk[None], (NE,) + chunk.shape),
        "expert",
        split_axis=0,
        concat_axis=0,
        tiled=True,
    ).reshape(LP, 3200)
    grad_query, grad_key, grad_value, grad_output, grad_router, rest_t = unpack(total_sum)
    grad_gain_two, grad_gain_one = rest_t[EXPERTS], rest_t[EXPERTS + 1]
    return (
        layer_output[None],
        grad_input[None],
        grad_gain_one,
        grad_query,
        grad_key,
        grad_value,
        grad_output,
        grad_router,
        grad_gain_two,
        grad_gate,
        grad_up,
        grad_down,
    )


def solution(mesh):
    placed = (
        P("expert", "fsdp", None),
        P("expert", None),
        P("expert", "fsdp", None),
        P("fsdp"),
        P("fsdp", None),
        P("fsdp", None),
        P("fsdp", None),
        P("fsdp", None),
        P("fsdp", None),
        P("fsdp"),
        P("expert", "fsdp", None),
        P("expert", "fsdp", None),
        P("expert", None, "fsdp"),
        P("expert", "fsdp", None),
    )
    return jax.shard_map(
        local,
        mesh=mesh,
        in_specs=placed,
        out_specs=(
            P("expert", "fsdp", None),
            P("expert", "fsdp", None),
            P("fsdp"),
            P("fsdp", None),
            P("fsdp", None),
            P("fsdp", None),
            P("fsdp", None),
            P("fsdp", None),
            P("fsdp"),
            P("expert", "fsdp", None),
            P("expert", "fsdp", None),
            P("expert", None, "fsdp"),
        ),
        check_vma=False,
    )
```

```python
import jax
import jax.numpy as jnp
import numpy as np
from jax import lax
from jax.experimental import pallas as pl
from jax.experimental.pallas import tpu as pltpu
from jax.sharding import PartitionSpec as P

HEAD_DIM = 64
EXPERTS = 32
SLOTS = 64
NF = 8
NE = 16
LP = 128
LENGTH = 1024
D = 1024
FF = 512

epsilon = 1e-06
rope_base = 10000.0
highest = lax.Precision.HIGHEST
bf16 = jnp.bfloat16
f32 = jnp.float32


def shift_x(v, k):
    return lax.ppermute(v, "fsdp", [(i, (i + 2 * k) % NF) for i in range(NF)])


def swap_core(v):
    return lax.ppermute(v, "fsdp", [(i, i ^ 1) for i in range(NF)])


def shift_z(v, k):
    return lax.ppermute(v, "expert", [(i, (i // 4) * 4 + (i + k) % 4) for i in range(NE)])


def shift_y(v, k):
    return lax.ppermute(v, "expert", [(i, (i + 4 * k) % NE) for i in range(NE)])


def put(buffer, piece, place):
    return lax.dynamic_update_index_in_dim(buffer, piece, place, 0)


def ring_gather(shift, v, place):
    got = [(v, place)] + [(shift(v, k), (place - k) % 4) for k in (1, 3, 2)]
    out = jnp.zeros((4,) + v.shape, v.dtype)
    for piece, where in got:
        out = put(out, piece, where)
    return out


def ring_gather_halves(shift, v, place):
    left, right = shift(v, 1), shift(v, 3)
    n = v.shape[0] // 2
    far = (shift(left[:n], 1), shift(right[n:], 3))
    out = jnp.zeros((4,) + v.shape, v.dtype)
    for piece, where in ((v, place), (left, (place - 1) % 4), (right, (place + 1) % 4)):
        out = put(out, piece, where)
    return put(out, jnp.concatenate(far, axis=0), (place + 2) % 4)


def gather_fsdp(v, beside=None):
    mine = ring_gather(shift_x, v, lax.axis_index("fsdp") // 2)
    if beside is not None:
        mine, beside = lax.optimization_barrier((mine, beside))
    return mine, swap_core(mine), beside


def in_order(mine, other):
    even = lax.axis_index("fsdp") % 2 == 0
    first = jnp.where(even, mine, other)
    second = jnp.where(even, other, mine)
    return jnp.stack([first, second], axis=1).reshape((NF * mine.shape[1],) + mine.shape[2:])


def gather_expert(v):
    e = lax.axis_index("expert")
    y, z = e // 4, e % 4
    n = v.shape[0] // 2
    a = ring_gather(shift_z, v[:n], z)
    b = ring_gather(shift_y, v[n:], y)
    return ring_gather_halves(shift_y, a, y), ring_gather_halves(shift_z, b, z)


def pieces_of(p, place):
    return [
        lax.dynamic_index_in_dim(p, (place + k) % 4, 0, keepdims=False) for k in range(4)
    ]


def ring_sum(shift, p, place):
    own, *others = pieces_of(p, place)
    total = own.astype(f32)
    for k in (1, 3, 2):
        total = total + shift(others[k - 1], k).astype(f32)
    return total


def ring_sum_halves(shift, p, place):
    own, right, far, left = pieces_of(p, place)
    n = own.shape[0] // 2
    from_left, from_right = shift(far[:n], 1), shift(far[n:], 3)
    right = jnp.concatenate([right[:n].astype(f32) + from_left.astype(f32), right[n:]], axis=0)
    left = jnp.concatenate([left[:n], left[n:].astype(f32) + from_right.astype(f32)], axis=0)
    total = own.astype(f32) + shift(right.astype(bf16), 1).astype(f32)
    return total + shift(left.astype(bf16), 3).astype(f32)


def scatter_expert(a, b, beside):
    e = lax.axis_index("expert")
    y, z = e // 4, e % 4
    a = ring_sum_halves(shift_y, a, y).astype(bf16)
    b = ring_sum_halves(shift_z, b, z).astype(bf16)
    a, b, beside = lax.optimization_barrier((a, b, beside))
    a = ring_sum(shift_z, a, z)
    b = ring_sum(shift_y, b, y)
    return jnp.concatenate([a, b], axis=0), beside


def pair_sum(p):
    c = lax.axis_index("fsdp") % 2
    p = p.reshape((4, 2) + p.shape[1:])
    kept = lax.dynamic_index_in_dim(p, c, 1, keepdims=False)
    given = lax.dynamic_index_in_dim(p, 1 - c, 1, keepdims=False)
    return (kept.astype(f32) + swap_core(given).astype(f32)).astype(bf16)


def after(v, first):
    return lax.optimization_barrier((v, first))[0]


def dot(a, b, dims=((1,), (0,))):
    return lax.dot_general(a, b, (dims, ((), ())), preferred_element_type=f32)


NT = ((1,), (1,))
TN = ((0,), (0,))


HALF = LP // 2


def expert_kernel(
    e_ref, rows_a, rows_b, cot, router, w, inputs, hidden, dboth, dres, mix, drows_a, drows_b
):
    e = e_ref[0]
    lane = lax.broadcasted_iota(jnp.int32, (1, 128), 1)
    ids = lax.broadcasted_iota(jnp.int32, (EXPERTS, LP), 0)
    ids_f = ids.astype(f32)
    slot_ids = lax.broadcasted_iota(jnp.int32, (SLOTS, LP), 0).astype(f32)
    earlier = (
        lax.broadcasted_iota(jnp.int32, (LP, LP), 0) < lax.broadcasted_iota(jnp.int32, (LP, LP), 1)
    ).astype(bf16)
    picks, gates, x_slots, c_slots = [], [], [], []
    for b in range(4):
        rows = jnp.concatenate([rows_a[0, b], rows_b[b, 0]], axis=0)
        routes = cot[b, LP:, :LP].astype(f32)
        has = routes[0:1] == ids_f
        for k in range(1, 8):
            has = has | (routes[k : k + 1] == ids_f)
        low = jnp.where(has, dot(router[...], rows, NT), -1e30)
        top = jnp.max(low, axis=0, keepdims=True)
        expo = jnp.where(has, jnp.exp(low - top), 0.0)
        soft = expo / jnp.sum(expo, axis=0, keepdims=True)
        pick_j, gate_j = [], []
        for j in range(2):
            here = ids == 2 * e + j
            member = jnp.sum(jnp.where(here & has, 1.0, 0.0), axis=0, keepdims=True)
            gate = jnp.sum(jnp.where(here, soft, 0.0), axis=0, keepdims=True)
            wide = jnp.broadcast_to(member, (16, LP)).astype(bf16)
            rank = dot(wide, earlier)[0:1]
            pick = jnp.where((rank == slot_ids) & (member > 0.5), 1.0, 0.0)
            pick_j.append(pick.astype(bf16))
            gate_j.append(jnp.sum(pick * gate, axis=1, keepdims=True))
        pick = jnp.concatenate(pick_j, axis=0)
        picks.append(pick)
        gates.append(gate_j)
        x_slots.append(dot(pick, rows).astype(bf16))
        c_slots.append(dot(pick, cot[b, :LP]))
    weighted, dassign, extra = [], [], []
    for j in range(2):
        part = slice(j * SLOTS, (j + 1) * SLOTS)
        x_in = jnp.concatenate([v[part] for v in x_slots], axis=0)
        c_in = jnp.concatenate([v[part] for v in c_slots], axis=0)
        gate_in = jnp.concatenate([v[j] for v in gates], axis=0)
        w_g = w[:, j * 1024 : j * 1024 + FF]
        w_u = w[:, j * 1024 + FF : (j + 1) * 1024]
        w_d = w[:, 2048 + j * FF : 2048 + (j + 1) * FF]
        gate_val = dot(x_in, w_g)
        up_val = dot(x_in, w_u)
        sig = 1.0 / (1.0 + jnp.exp(-gate_val))
        activated = gate_val * sig
        hid = (activated * up_val).astype(bf16)
        result = dot(hid, w_d, NT).astype(bf16).astype(f32)
        dgate = jnp.sum(result * c_in, axis=-1, keepdims=True)
        dresult = (gate_in * c_in).astype(bf16)
        dhidden = dot(dresult, w_d)
        dgate_val = (dhidden * up_val * sig * (1.0 + gate_val * (1.0 - sig))).astype(bf16)
        dup_val = (dhidden * activated).astype(bf16)
        da = (dot(dgate_val, w_g, NT) + dot(dup_val, w_u, NT)).astype(bf16)
        weighted.append((gate_in * result).astype(bf16))
        dassign.append(da)
        dg_high = dgate.astype(bf16).astype(f32)
        dg_low = dgate - dg_high
        extra.append(
            (
                jnp.where(lane == 2 * e + j, dg_high, 0.0)
                + jnp.where(lane == EXPERTS + 2 * e + j, dg_low, 0.0)
            ).astype(bf16)
        )
        inputs[j] = x_in
        hidden[j] = hid
        dboth[j, :, :FF] = dgate_val
        dboth[j, :, FF:] = dup_val
        dres[j] = dresult
    for b in range(4):
        part = slice(b * SLOTS, (b + 1) * SLOTS)
        weighted_b = jnp.concatenate([weighted[0][part], weighted[1][part]], axis=0)
        dassign_b = jnp.concatenate([dassign[0][part], dassign[1][part]], axis=0)
        extra_b = jnp.concatenate([extra[0][part], extra[1][part]], axis=0)
        mix[b] = dot(picks[b], weighted_b, TN).astype(bf16)
        d_rows = dot(picks[b], dassign_b, TN).astype(bf16)
        d_extra = dot(picks[b], extra_b, TN).astype(bf16)
        drows_a[0, b, :, :D] = d_rows[:HALF]
        drows_a[0, b, :, D:] = d_extra[:HALF]
        drows_b[b, 0, :, :D] = d_rows[HALF:]
        drows_b[b, 0, :, D:] = d_extra[HALF:]


def experts(e, rows_a, rows_b, cot_all, router, w):
    rows = NE * SLOTS
    step = rows // 4
    return pl.pallas_call(
        expert_kernel,
        grid=(4,),
        in_specs=[
            pl.BlockSpec(memory_space=pltpu.SMEM),
            pl.BlockSpec((1, 4, HALF, D), lambda i: (i, 0, 0, 0)),
            pl.BlockSpec((4, 1, HALF, D), lambda i: (0, i, 0, 0)),
            pl.BlockSpec((4, LP + 16, D), lambda i: (i, 0, 0)),
            pl.BlockSpec((EXPERTS, D), lambda i: (0, 0)),
            pl.BlockSpec((D, 3072), lambda i: (0, 0), pipeline_mode=pl.Buffered(1)),
        ],
        out_specs=[
            pl.BlockSpec((2, step, D), lambda i: (0, i, 0)),
            pl.BlockSpec((2, step, FF), lambda i: (0, i, 0)),
            pl.BlockSpec((2, step, 2 * FF), lambda i: (0, i, 0)),
            pl.BlockSpec((2, step, D), lambda i: (0, i, 0)),
            pl.BlockSpec((4, LP, D), lambda i: (i, 0, 0)),
            pl.BlockSpec((1, 4, HALF, D + 128), lambda i: (i, 0, 0, 0)),
            pl.BlockSpec((4, 1, HALF, D + 128), lambda i: (0, i, 0, 0)),
        ],
        out_shape=[
            jax.ShapeDtypeStruct((2, rows, D), bf16),
            jax.ShapeDtypeStruct((2, rows, FF), bf16),
            jax.ShapeDtypeStruct((2, rows, 2 * FF), bf16),
            jax.ShapeDtypeStruct((2, rows, D), bf16),
            jax.ShapeDtypeStruct((NE, LP, D), bf16),
            jax.ShapeDtypeStruct((4, 4, HALF, D + 128), bf16),
            jax.ShapeDtypeStruct((4, 4, HALF, D + 128), bf16),
        ],
        compiler_params=pltpu.CompilerParams(vmem_limit_bytes=56 * 2**20),
        cost_estimate=pl.CostEstimate(
            flops=14 * 10**9, bytes_accessed=30 * 2**20, transcendentals=10**6
        ),
        name="experts",
    )(e, rows_a, rows_b, cot_all, router, w)


def weight_kernel(inputs, dres, dboth, hidden, out):
    for j in range(2):
        out[:, :, j * 1024 : (j + 1) * 1024] = (
            dot(inputs[j], dboth[j], TN).astype(bf16).reshape(2, LP, 1024)
        )
        out[:, :, 2048 + j * FF : 2048 + (j + 1) * FF] = (
            dot(dres[j], hidden[j], TN).astype(bf16).reshape(2, LP, FF)
        )


def expert_weights(inputs, dres, dboth, hidden):
    rows = NE * SLOTS
    return pl.pallas_call(
        weight_kernel,
        grid=(4,),
        in_specs=[
            pl.BlockSpec((2, rows, 256), lambda i: (0, 0, i)),
            pl.BlockSpec((2, rows, 256), lambda i: (0, 0, i)),
            pl.BlockSpec((2, rows, 2 * FF), lambda i: (0, 0, 0)),
            pl.BlockSpec((2, rows, FF), lambda i: (0, 0, 0)),
        ],
        out_specs=pl.BlockSpec((2, LP, 3072), lambda i: (i, 0, 0)),
        out_shape=jax.ShapeDtypeStruct((NF, LP, 3072), bf16),
        compiler_params=pltpu.CompilerParams(vmem_limit_bytes=56 * 2**20),
        cost_estimate=pl.CostEstimate(
            flops=7 * 10**9, bytes_accessed=20 * 2**20, transcendentals=0
        ),
        name="expert_weights",
    )(inputs, dres, dboth, hidden)


def swap_fsdp(v):
    return lax.all_to_all(v, "fsdp", split_axis=0, concat_axis=0, tiled=True)


def rope_tables():
    exponent = np.arange(HEAD_DIM // 2, dtype=np.float32) * np.float32(2.0 / HEAD_DIM)
    inverse = np.power(np.float32(rope_base), -exponent).astype(np.float32)
    angles = np.arange(LENGTH, dtype=np.float32)[:, None] * inverse[None, :]
    wide = np.tile(angles.astype(np.float32), (1, 4))
    return np.cos(wide).astype(np.float32), np.sin(wide).astype(np.float32)


def masked_gates(logits, member):
    low = jnp.where(member, logits, -1e30)
    top = jnp.max(low, axis=-1, keepdims=True)
    expo = jnp.where(member, jnp.exp(low - top), 0.0)
    return expo / jnp.sum(expo, axis=-1, keepdims=True)


def norm_back(u, v, gain):
    r = lax.rsqrt(jnp.mean(v * v, axis=-1, keepdims=True) + epsilon)
    inner = jnp.mean(gain * u * v, axis=-1, keepdims=True)
    return r * gain * u - v * (r * r * r) * inner, jnp.sum(u * v * r, axis=0)


def masked_scores(q_h, keys, seg_col, seg_row, first):
    rows, count = q_h.shape[0], keys.shape[0]
    scores = dot(q_h, keys, NT) * HEAD_DIM**-0.5
    row = lax.broadcasted_iota(jnp.int32, (rows, count), 0) + first
    column = lax.broadcasted_iota(jnp.int32, (rows, count), 1)
    allowed = (seg_col == seg_row) & (column <= row)
    return jnp.where(allowed, scores, -1e30)


QB = 256


def order_rows(core, mine, other, out):
    for x in range(4):
        own = pl.multiple_of(x * 2 * LP + core * LP, LP)
        out[pl.ds(own, LP)] = mine[x]
        beside = pl.multiple_of(x * 2 * LP + (1 - core) * LP, LP)
        out[pl.ds(beside, LP)] = other[x]


def pack_kernel(w_query, w_key, w_value, w_router, gains, out):
    rest = jnp.concatenate(
        [w_router[...], gains[...], jnp.zeros((LP, 128 - EXPERTS - 2), bf16)], axis=1
    )
    for f in range(NF):
        out[f, :, :128] = w_query[:, f * 128 : (f + 1) * 128]
        out[f, :, 128:192] = w_key[:, f * 64 : (f + 1) * 64]
        out[f, :, 192:256] = w_value[:, f * 64 : (f + 1) * 64]
        out[f, :, 256:] = rest


def pack(*operands):
    return pl.pallas_call(
        pack_kernel,
        out_shape=jax.ShapeDtypeStruct((NF, LP, 384), bf16),
        cost_estimate=pl.CostEstimate(flops=10**6, bytes_accessed=2 * 2**20, transcendentals=0),
        name="pack",
    )(*operands)


def half_swap(v):
    lane = lax.broadcasted_iota(jnp.int32, v.shape, 1)
    return jnp.where(lane % 64 < 32, -pltpu.roll(v, 96, 1), pltpu.roll(v, 32, 1))


def attend_kernel(
    core,
    mine,
    other,
    got,
    cos,
    sin,
    seg_col,
    seg_row,
    x,
    normed,
    qkv,
    attended,
    attended_send,
    lse,
    rest,
):
    order_rows(core[0], mine, other, x)
    for f in range(NF):
        part = slice(f * LP, (f + 1) * LP)
        rest[:, part] = jnp.transpose(got[part, 256:].astype(f32))[: EXPERTS + 8]
    x_full = x[...].astype(f32)
    r = lax.rsqrt(jnp.mean(x_full * x_full, axis=-1, keepdims=True) + epsilon)
    normed[...] = (x_full * r * rest[EXPERTS : EXPERTS + 1]).astype(bf16)
    raw = dot(normed[...], got[:, :256])
    turned = lax.broadcasted_iota(jnp.int32, (1, 128), 1) < HEAD_DIM
    cos_k, sin_k = jnp.where(turned, cos[...], 1.0), jnp.where(turned, sin[...], 0.0)
    raw_q, raw_kv = raw[:, :128], raw[:, 128:]
    qkv[:, :128] = (raw_q * cos[...] + half_swap(raw_q) * sin[...]).astype(bf16)
    qkv[:, 128:] = (raw_kv * cos_k + half_swap(raw_kv) * sin_k).astype(bf16)
    for i in range(LENGTH // QB):
        part, count = slice(i * QB, (i + 1) * QB), (i + 1) * QB
        keys, values = qkv[:count, 128:192], qkv[:count, 192:256]
        for h in range(2):
            scores = masked_scores(
                qkv[part, h * 64 : (h + 1) * 64], keys, seg_col[part], seg_row[:, :count], i * QB
            )
            top = jnp.max(scores, axis=-1, keepdims=True)
            expo = jnp.exp(scores - top)
            total = jnp.sum(expo, axis=-1, keepdims=True)
            probs = (expo * (1.0 / total)).astype(bf16)
            attended[part, h * 64 : (h + 1) * 64] = dot(probs, values).astype(bf16)
            lse[part, h : h + 1] = top + jnp.log(total)
        attended_send[2 * i : 2 * i + 2] = attended[part].reshape(2, LP, 128)


VMEM = pl.BlockSpec(memory_space=pltpu.VMEM)
SMEM = pl.BlockSpec(memory_space=pltpu.SMEM)


def attend(*operands):
    return pl.pallas_call(
        attend_kernel,
        in_specs=[SMEM] + [VMEM] * (len(operands) - 1),
        out_shape=[
            jax.ShapeDtypeStruct((LENGTH, D), bf16),
            jax.ShapeDtypeStruct((LENGTH, D), bf16),
            jax.ShapeDtypeStruct((LENGTH, 256), bf16),
            jax.ShapeDtypeStruct((LENGTH, 128), bf16),
            jax.ShapeDtypeStruct((NF, LP, 128), bf16),
            jax.ShapeDtypeStruct((LENGTH, 2), f32),
            jax.ShapeDtypeStruct((EXPERTS + 8, D), f32),
        ],
        compiler_params=pltpu.CompilerParams(vmem_limit_bytes=56 * 2**20),
        cost_estimate=pl.CostEstimate(
            flops=3 * 10**9, bytes_accessed=6 * 2**20, transcendentals=2 * 10**6
        ),
        name="attend",
    )(*operands)


def branch_back_kernel(core, mine, other, w_out, attended, part_output, dout, dbranch):
    order_rows(core[0], mine, other, dbranch)
    part_output[...] = dot(attended[...], dbranch[...], TN).astype(bf16)
    dout[...] = dot(dbranch[...], w_out[...], NT).astype(bf16)


def branch_back(*operands):
    return pl.pallas_call(
        branch_back_kernel,
        in_specs=[SMEM] + [VMEM] * (len(operands) - 1),
        out_shape=[
            jax.ShapeDtypeStruct((LP, D), bf16),
            jax.ShapeDtypeStruct((LENGTH, 128), bf16),
        ],
        scratch_shapes=[pltpu.VMEM((LENGTH, D), bf16)],
        compiler_params=pltpu.CompilerParams(vmem_limit_bytes=14 * 2**20),
        cost_estimate=pl.CostEstimate(
            flops=6 * 10**8, bytes_accessed=5 * 2**20, transcendentals=0
        ),
        name="branch_back",
    )(*operands)


def attend_back_kernel(
    x, normed, got, qkv, lse, dout, extra, cos, sin, seg_col, seg_row, payload, dnormed, dq, dkv
):
    dkv[...] = jnp.zeros_like(dkv)
    scale = HEAD_DIM**-0.5
    for i in range(LENGTH // QB):
        part, count = slice(i * QB, (i + 1) * QB), (i + 1) * QB
        keys, values = qkv[:count, 128:192], qkv[:count, 192:256]
        dk_part, dv_part = 0.0, 0.0
        for h in range(2):
            q_h, do_h = qkv[part, h * 64 : (h + 1) * 64], dout[part, h * 64 : (h + 1) * 64]
            scores = masked_scores(q_h, keys, seg_col[part], seg_row[:, :count], i * QB)
            probs = jnp.exp(scores - lse[part, h : h + 1])
            dprobs = dot(do_h, values, NT)
            delta = jnp.sum(probs * dprobs, axis=-1, keepdims=True)
            dscores = (probs * (dprobs - delta)).astype(bf16)
            dq[part, h * 64 : (h + 1) * 64] = dot(dscores, keys) * scale
            dk_part = dk_part + dot(dscores, q_h, TN)
            dv_part = dv_part + dot(probs.astype(bf16), do_h, TN)
        dkv[:count, :64] += dk_part * scale
        dkv[:count, 64:] += dv_part
    d_q, d_kv = dq[...], dkv[...]
    turned = lax.broadcasted_iota(jnp.int32, (1, 128), 1) < HEAD_DIM
    cos_k, sin_k = jnp.where(turned, cos[...], 1.0), jnp.where(turned, sin[...], 0.0)
    d_q = (d_q * cos[...] - half_swap(d_q) * sin[...]).astype(bf16)
    d_kv = (d_kv * cos_k - half_swap(d_kv) * sin_k).astype(bf16)
    dqkv = jnp.concatenate([d_q, d_kv], axis=1)
    payload[:, :256] = dot(normed[...], dqkv, TN).astype(bf16)
    d_n = dot(dqkv, got[:, :256], NT)
    dnormed[...] = d_n.astype(bf16).reshape(NF, LP, D)
    x_full = x[...].astype(f32)
    r = lax.rsqrt(jnp.mean(x_full * x_full, axis=-1, keepdims=True) + epsilon)
    dgain = jnp.sum(d_n * (x_full * r), axis=0, keepdims=True)
    lane = lax.broadcasted_iota(jnp.int32, (LP, 128), 1)
    for f in range(NF):
        part = slice(f * LP, (f + 1) * LP)
        column = jnp.transpose(jnp.broadcast_to(dgain[:, part], (128, LP)))
        payload[part, 256:] = jnp.where(
            lane == EXPERTS + 1, column, extra[part].astype(f32)
        ).astype(bf16)


def attend_back(*operands):
    return pl.pallas_call(
        attend_back_kernel,
        out_shape=[
            jax.ShapeDtypeStruct((LENGTH, 384), bf16),
            jax.ShapeDtypeStruct((NF, LP, D), bf16),
        ],
        scratch_shapes=[
            pltpu.VMEM((LENGTH, 128), f32),
            pltpu.VMEM((LENGTH, 128), f32),
        ],
        compiler_params=pltpu.CompilerParams(vmem_limit_bytes=56 * 2**20),
        cost_estimate=pl.CostEstimate(
            flops=6 * 10**9, bytes_accessed=14 * 2**20, transcendentals=2 * 10**6
        ),
        name="attend_back",
    )(*operands)


def unpack_kernel(
    total, grads, query, key, value, output, router_t, gain_two, gain_one, gate, up, down
):
    query[...] = total[:, :1024].astype(f32)
    key[...] = total[:, 1024:1536].astype(f32)
    value[...] = total[:, 1536:2048].astype(f32)
    output[...] = total[:, 2176:].astype(f32)
    rest_t = jnp.transpose(total[:, 2048:2176].astype(f32))
    router_t[...] = rest_t[:EXPERTS]
    gain_two[...] = rest_t[EXPERTS : EXPERTS + 1]
    gain_one[...] = rest_t[EXPERTS + 1 : EXPERTS + 2]
    for j in range(2):
        gate[j] = grads[:, j * 1024 : j * 1024 + FF].astype(f32)
        up[j] = grads[:, j * 1024 + FF : (j + 1) * 1024].astype(f32)
        down[j] = jnp.transpose(grads[:, 2048 + j * FF : 2048 + (j + 1) * FF].astype(f32))


def unpack(total, grads):
    shapes = [(LP, D), (LP, FF), (LP, FF), (LP, D), (EXPERTS, LP), (1, LP), (1, LP)]
    shapes += [(2, LP, FF), (2, LP, FF), (2, FF, LP)]
    return pl.pallas_call(
        unpack_kernel,
        out_shape=[jax.ShapeDtypeStruct(shape, f32) for shape in shapes],
        cost_estimate=pl.CostEstimate(flops=10**6, bytes_accessed=6 * 2**20, transcendentals=0),
        name="unpack",
    )(total, grads)


HEAD_PARTS = (slice(0, 128), slice(128, 192), slice(192, 256))


def local(
    layer_input,
    segment_ids,
    routes,
    attn_gain,
    w_query,
    w_key,
    w_value,
    w_output,
    w_router,
    ffn_gain,
    w_gate,
    w_up,
    w_down,
    cotangent,
):
    e = lax.axis_index("expert")
    x_own = layer_input[0]
    cot_own = cotangent[0]
    payload = pack(
        w_query, w_key, w_value, w_router, jnp.stack([attn_gain, ffn_gain], axis=1)
    )
    core = (lax.axis_index("fsdp") % 2)[None]
    x_mine, x_other, got = gather_fsdp(x_own, swap_fsdp(payload))
    got = got.reshape(D, 384)
    cot_all = lax.all_gather(
        jnp.concatenate(
            [
                cot_own,
                jnp.pad(routes[0].astype(bf16).T, ((0, 8), (0, D - LP))),
            ],
            axis=0,
        ),
        "expert",
        axis=0,
    )

    cos_wide, sin_wide = (jnp.asarray(table) for table in rope_tables())
    seg_row = segment_ids
    seg_col = segment_ids.reshape(LENGTH, 1)
    x_all, normed, qkv, attended, attended_send, lse, rest = attend(
        core, x_mine, x_other, got, cos_wide, sin_wide, seg_col, seg_row
    )
    router_t = rest[:EXPERTS].astype(bf16)
    gain_one, gain_two = rest[EXPERTS], rest[EXPERTS + 1]
    w_mine, w_other, attended_send = gather_fsdp(after(w_output, x_other), attended_send)
    w_out = in_order(w_mine, w_other)
    member_own = jnp.any(
        routes[0][:, :, None] == jnp.arange(EXPERTS, dtype=jnp.int32), axis=1
    )

    attended_own = swap_fsdp(attended_send).swapaxes(0, 1).reshape(LP, D)
    w_own = jnp.concatenate(
        [w_gate[0], w_up[0], w_gate[1], w_up[1], w_down[0].T, w_down[1].T], axis=1
    )
    w_own = after(w_own, attended_own)
    w_exp = lax.all_gather(w_own, "fsdp", axis=0, tiled=True)
    after_attn = x_own.astype(f32) + jnp.dot(attended_own, w_out, preferred_element_type=f32)
    r_two = lax.rsqrt(jnp.mean(after_attn * after_attn, axis=-1, keepdims=True) + epsilon)
    normed_two = (after_attn * r_two * gain_two).astype(bf16)

    rows_a, rows_b = gather_expert(normed_two)
    inputs, hidden, dboth, dres, mix_part, drows_a, drows_b = experts(
        e[None], rows_a, rows_b, cot_all, router_t, w_exp
    )
    mix = lax.psum_scatter(mix_part, "expert", scatter_dimension=0)
    grad_exp = expert_weights(inputs, dres, dboth, hidden)
    drows, grad_exp = scatter_expert(drows_a, drows_b, grad_exp)
    grad_exp = lax.psum_scatter(grad_exp, "fsdp", scatter_dimension=0)

    logits = jnp.einsum("td,ed->te", normed_two, router_t, preferred_element_type=f32)
    gates = masked_gates(logits, member_own)
    dgate_own = drows[:, D : D + EXPERTS] + drows[:, D + EXPERTS : D + 2 * EXPERTS]
    dlogits = gates * (dgate_own - jnp.sum(gates * dgate_own, axis=-1, keepdims=True))
    dnormed_two = drows[:, :D] + jnp.einsum(
        "te,ed->td", dlogits, router_t.astype(f32), precision=highest
    )
    dafter_norm, part_gain_two = norm_back(dnormed_two, after_attn, gain_two)
    dafter = cot_own.astype(f32) + dafter_norm
    dbranch = dafter.astype(bf16)
    d_mine, d_other, _ = gather_fsdp(dbranch)
    part_router = jnp.einsum(
        "td,te->de", normed_two.astype(f32), dlogits, precision=highest
    )

    extra = jnp.concatenate(
        [
            part_router.astype(bf16),
            part_gain_two[:, None].astype(bf16),
            jnp.zeros((D, 128 - EXPERTS - 1), bf16),
        ],
        axis=-1,
    )

    part_output, dout = branch_back(core, d_mine, d_other, w_output, attended)
    part_output = lax.all_to_all(
        part_output.reshape(NE, LP // NE, D), "expert", split_axis=0, concat_axis=0, tiled=True
    )
    payload, dnormed_part = attend_back(
        x_all, normed, got, qkv, lse, dout, extra, cos_wide, sin_wide, seg_col, seg_row
    )
    payload, dnormed_part, mix, part_output = lax.optimization_barrier(
        (payload, dnormed_part, mix, part_output)
    )
    layer_output = (after_attn + mix.astype(f32)).astype(bf16)
    dnormed_pair = pair_sum(dnormed_part)
    small = lax.all_to_all(
        payload.reshape(NF * NE, LP // NE, 384),
        ("fsdp", "expert"),
        split_axis=0,
        concat_axis=0,
        tiled=True,
    )
    small = jnp.sum(small.reshape(NF, NE, LP // NE, 384).astype(f32), axis=1)
    chunk_output = jnp.sum(part_output.astype(f32), axis=0)
    chunk = jnp.concatenate(
        [small[:, :, part].swapaxes(0, 1).reshape(LP // NE, -1) for part in HEAD_PARTS]
        + [jnp.sum(small[:, :, 256:], axis=0), chunk_output],
        axis=-1,
    ).astype(bf16)
    chunk, dnormed_pair = lax.optimization_barrier((chunk, dnormed_pair))
    total_sum = lax.all_to_all(
        jnp.broadcast_to(chunk[None], (NE,) + chunk.shape),
        "expert",
        split_axis=0,
        concat_axis=0,
        tiled=True,
    ).reshape(LP, 3200)
    dnormed = ring_sum(shift_x, dnormed_pair, lax.axis_index("fsdp") // 2)
    dinput_norm, _ = norm_back(dnormed, x_own.astype(f32), gain_one)
    grad_input = (dafter + dinput_norm).astype(bf16)
    (
        grad_query,
        grad_key,
        grad_value,
        grad_output,
        grad_router_t,
        grad_gain_two,
        grad_gain_one,
        grad_gate,
        grad_up,
        grad_down,
    ) = unpack(total_sum, grad_exp)
    return (
        layer_output[None],
        grad_input[None],
        grad_gain_one.reshape(LP),
        grad_query,
        grad_key,
        grad_value,
        grad_output,
        grad_router_t.T,
        grad_gain_two.reshape(LP),
        grad_gate,
        grad_up,
        grad_down,
    )


def solution(mesh):
    placed = (
        P("expert", "fsdp", None),
        P("expert", None),
        P("expert", "fsdp", None),
        P("fsdp"),
        P("fsdp", None),
        P("fsdp", None),
        P("fsdp", None),
        P("fsdp", None),
        P("fsdp", None),
        P("fsdp"),
        P("expert", "fsdp", None),
        P("expert", "fsdp", None),
        P("expert", None, "fsdp"),
        P("expert", "fsdp", None),
    )
    return jax.shard_map(
        local,
        mesh=mesh,
        in_specs=placed,
        out_specs=(
            P("expert", "fsdp", None),
            P("expert", "fsdp", None),
            P("fsdp"),
            P("fsdp", None),
            P("fsdp", None),
            P("fsdp", None),
            P("fsdp", None),
            P("fsdp", None),
            P("fsdp"),
            P("expert", "fsdp", None),
            P("expert", "fsdp", None),
            P("expert", None, "fsdp"),
        ),
        check_vma=False,
    )
```

```python
import jax
import jax.numpy as jnp
import numpy as np
from jax import lax
from jax.experimental import pallas as pl
from jax.experimental.pallas import tpu as pltpu
from jax.sharding import PartitionSpec as P

HEAD_DIM = 64
EXPERTS = 32
SLOTS = 64
NF = 8
NE = 16
LP = 128
LENGTH = 1024
D = 1024
FF = 512

epsilon = 1e-06
rope_base = 10000.0
highest = lax.Precision.HIGHEST
bf16 = jnp.bfloat16
f32 = jnp.float32


def shift_x(v, k):
    return lax.ppermute(v, "fsdp", [(i, (i + 2 * k) % NF) for i in range(NF)])


def swap_core(v):
    return lax.ppermute(v, "fsdp", [(i, i ^ 1) for i in range(NF)])


def shift_z(v, k):
    return lax.ppermute(v, "expert", [(i, (i // 4) * 4 + (i + k) % 4) for i in range(NE)])


def shift_y(v, k):
    return lax.ppermute(v, "expert", [(i, (i + 4 * k) % NE) for i in range(NE)])


def put(buffer, piece, place):
    return lax.dynamic_update_index_in_dim(buffer, piece, place, 0)


def ring_gather(shift, v, place):
    got = [(v, place)] + [(shift(v, k), (place - k) % 4) for k in (1, 3, 2)]
    out = jnp.zeros((4,) + v.shape, v.dtype)
    for piece, where in got:
        out = put(out, piece, where)
    return out


def ring_gather_halves(shift, v, place):
    left, right = shift(v, 1), shift(v, 3)
    n = v.shape[0] // 2
    far = (shift(left[:n], 1), shift(right[n:], 3))
    out = jnp.zeros((4,) + v.shape, v.dtype)
    for piece, where in ((v, place), (left, (place - 1) % 4), (right, (place + 1) % 4)):
        out = put(out, piece, where)
    return put(out, jnp.concatenate(far, axis=0), (place + 2) % 4)


def gather_fsdp(v, beside=None):
    mine = ring_gather(shift_x, v, lax.axis_index("fsdp") // 2)
    if beside is not None:
        mine, beside = lax.optimization_barrier((mine, beside))
    return mine, swap_core(mine), beside


def in_order(mine, other):
    even = lax.axis_index("fsdp") % 2 == 0
    first = jnp.where(even, mine, other)
    second = jnp.where(even, other, mine)
    return jnp.stack([first, second], axis=1).reshape((NF * mine.shape[1],) + mine.shape[2:])


def gather_expert(v):
    e = lax.axis_index("expert")
    y, z = e // 4, e % 4
    n = v.shape[0] // 2
    a = ring_gather(shift_z, v[:n], z)
    b = ring_gather(shift_y, v[n:], y)
    return ring_gather_halves(shift_y, a, y), ring_gather_halves(shift_z, b, z)


def pieces_of(p, place):
    return [
        lax.dynamic_index_in_dim(p, (place + k) % 4, 0, keepdims=False) for k in range(4)
    ]


def ring_sum(shift, p, place):
    own, *others = pieces_of(p, place)
    total = own.astype(f32)
    for k in (1, 3, 2):
        total = total + shift(others[k - 1], k).astype(f32)
    return total


def ring_sum_halves(shift, p, place):
    own, right, far, left = pieces_of(p, place)
    n = own.shape[0] // 2
    from_left, from_right = shift(far[:n], 1), shift(far[n:], 3)
    right = jnp.concatenate([right[:n].astype(f32) + from_left.astype(f32), right[n:]], axis=0)
    left = jnp.concatenate([left[:n], left[n:].astype(f32) + from_right.astype(f32)], axis=0)
    total = own.astype(f32) + shift(right.astype(bf16), 1).astype(f32)
    return total + shift(left.astype(bf16), 3).astype(f32)


def scatter_expert(a, b, beside):
    e = lax.axis_index("expert")
    y, z = e // 4, e % 4
    a = ring_sum_halves(shift_y, a, y).astype(bf16)
    b = ring_sum_halves(shift_z, b, z).astype(bf16)
    a, b, beside = lax.optimization_barrier((a, b, beside))
    a = ring_sum(shift_z, a, z)
    b = ring_sum(shift_y, b, y)
    return jnp.concatenate([a, b], axis=0), beside


def pair_sum(p):
    c = lax.axis_index("fsdp") % 2
    p = p.reshape((4, 2) + p.shape[1:])
    kept = lax.dynamic_index_in_dim(p, c, 1, keepdims=False)
    given = lax.dynamic_index_in_dim(p, 1 - c, 1, keepdims=False)
    return (kept.astype(f32) + swap_core(given).astype(f32)).astype(bf16)


def after(v, first):
    return lax.optimization_barrier((v, first))[0]


def dot(a, b, dims=((1,), (0,))):
    return lax.dot_general(a, b, (dims, ((), ())), preferred_element_type=f32)


NT = ((1,), (1,))
TN = ((0,), (0,))


HALF = LP // 2


def expert_kernel(
    e_ref, rows_a, rows_b, cot, router, w, inputs, hidden, dboth, dres, mix, drows_a, drows_b
):
    e = e_ref[0]
    lane = lax.broadcasted_iota(jnp.int32, (1, 128), 1)
    ids = lax.broadcasted_iota(jnp.int32, (EXPERTS, LP), 0)
    ids_f = ids.astype(f32)
    slot_ids = lax.broadcasted_iota(jnp.int32, (SLOTS, LP), 0).astype(f32)
    earlier = (
        lax.broadcasted_iota(jnp.int32, (LP, LP), 0) < lax.broadcasted_iota(jnp.int32, (LP, LP), 1)
    ).astype(bf16)
    picks, gates, x_slots, c_slots = [], [], [], []
    for b in range(4):
        rows = jnp.concatenate([rows_a[0, b], rows_b[b, 0]], axis=0)
        routes = cot[b, LP:, :LP].astype(f32)
        has = routes[0:1] == ids_f
        for k in range(1, 8):
            has = has | (routes[k : k + 1] == ids_f)
        low = jnp.where(has, dot(router[...], rows, NT), -1e30)
        top = jnp.max(low, axis=0, keepdims=True)
        expo = jnp.where(has, jnp.exp(low - top), 0.0)
        soft = expo / jnp.sum(expo, axis=0, keepdims=True)
        pick_j, gate_j = [], []
        for j in range(2):
            here = ids == 2 * e + j
            member = jnp.sum(jnp.where(here & has, 1.0, 0.0), axis=0, keepdims=True)
            gate = jnp.sum(jnp.where(here, soft, 0.0), axis=0, keepdims=True)
            wide = jnp.broadcast_to(member, (16, LP)).astype(bf16)
            rank = dot(wide, earlier)[0:1]
            pick = jnp.where((rank == slot_ids) & (member > 0.5), 1.0, 0.0)
            pick_j.append(pick.astype(bf16))
            gate_j.append(jnp.sum(pick * gate, axis=1, keepdims=True))
        pick = jnp.concatenate(pick_j, axis=0)
        picks.append(pick)
        gates.append(gate_j)
        x_slots.append(dot(pick, rows).astype(bf16))
        c_slots.append(dot(pick, cot[b, :LP]))
    weighted, dassign, extra = [], [], []
    for j in range(2):
        part = slice(j * SLOTS, (j + 1) * SLOTS)
        x_in = jnp.concatenate([v[part] for v in x_slots], axis=0)
        c_in = jnp.concatenate([v[part] for v in c_slots], axis=0)
        gate_in = jnp.concatenate([v[j] for v in gates], axis=0)
        w_g = w[:, j * 1024 : j * 1024 + FF]
        w_u = w[:, j * 1024 + FF : (j + 1) * 1024]
        w_d = w[:, 2048 + j * FF : 2048 + (j + 1) * FF]
        gate_val = dot(x_in, w_g)
        up_val = dot(x_in, w_u)
        sig = 1.0 / (1.0 + jnp.exp(-gate_val))
        activated = gate_val * sig
        hid = (activated * up_val).astype(bf16)
        result = dot(hid, w_d, NT).astype(bf16).astype(f32)
        dgate = jnp.sum(result * c_in, axis=-1, keepdims=True)
        dresult = (gate_in * c_in).astype(bf16)
        dhidden = dot(dresult, w_d)
        dgate_val = (dhidden * up_val * sig * (1.0 + gate_val * (1.0 - sig))).astype(bf16)
        dup_val = (dhidden * activated).astype(bf16)
        da = (dot(dgate_val, w_g, NT) + dot(dup_val, w_u, NT)).astype(bf16)
        weighted.append((gate_in * result).astype(bf16))
        dassign.append(da)
        dg_high = dgate.astype(bf16).astype(f32)
        dg_low = dgate - dg_high
        extra.append(
            (
                jnp.where(lane == 2 * e + j, dg_high, 0.0)
                + jnp.where(lane == EXPERTS + 2 * e + j, dg_low, 0.0)
            ).astype(bf16)
        )
        inputs[j] = x_in
        hidden[j] = hid
        dboth[j, :, :FF] = dgate_val
        dboth[j, :, FF:] = dup_val
        dres[j] = dresult
    for b in range(4):
        part = slice(b * SLOTS, (b + 1) * SLOTS)
        weighted_b = jnp.concatenate([weighted[0][part], weighted[1][part]], axis=0)
        dassign_b = jnp.concatenate([dassign[0][part], dassign[1][part]], axis=0)
        extra_b = jnp.concatenate([extra[0][part], extra[1][part]], axis=0)
        mix[b] = dot(picks[b], weighted_b, TN).astype(bf16)
        d_rows = dot(picks[b], dassign_b, TN).astype(bf16)
        d_extra = dot(picks[b], extra_b, TN).astype(bf16)
        drows_a[0, b, :, :D] = d_rows[:HALF]
        drows_a[0, b, :, D:] = d_extra[:HALF]
        drows_b[b, 0, :, :D] = d_rows[HALF:]
        drows_b[b, 0, :, D:] = d_extra[HALF:]


def experts(e, rows_a, rows_b, cot_all, router, w):
    rows = NE * SLOTS
    step = rows // 4
    return pl.pallas_call(
        expert_kernel,
        grid=(4,),
        in_specs=[
            pl.BlockSpec(memory_space=pltpu.SMEM),
            pl.BlockSpec((1, 4, HALF, D), lambda i: (i, 0, 0, 0)),
            pl.BlockSpec((4, 1, HALF, D), lambda i: (0, i, 0, 0)),
            pl.BlockSpec((4, LP + 16, D), lambda i: (i, 0, 0)),
            pl.BlockSpec((EXPERTS, D), lambda i: (0, 0)),
            pl.BlockSpec((D, 3072), lambda i: (0, 0), pipeline_mode=pl.Buffered(1)),
        ],
        out_specs=[
            pl.BlockSpec((2, step, D), lambda i: (0, i, 0)),
            pl.BlockSpec((2, step, FF), lambda i: (0, i, 0)),
            pl.BlockSpec((2, step, 2 * FF), lambda i: (0, i, 0)),
            pl.BlockSpec((2, step, D), lambda i: (0, i, 0)),
            pl.BlockSpec((4, LP, D), lambda i: (i, 0, 0)),
            pl.BlockSpec((1, 4, HALF, D + 128), lambda i: (i, 0, 0, 0)),
            pl.BlockSpec((4, 1, HALF, D + 128), lambda i: (0, i, 0, 0)),
        ],
        out_shape=[
            jax.ShapeDtypeStruct((2, rows, D), bf16),
            jax.ShapeDtypeStruct((2, rows, FF), bf16),
            jax.ShapeDtypeStruct((2, rows, 2 * FF), bf16),
            jax.ShapeDtypeStruct((2, rows, D), bf16),
            jax.ShapeDtypeStruct((NE, LP, D), bf16),
            jax.ShapeDtypeStruct((4, 4, HALF, D + 128), bf16),
            jax.ShapeDtypeStruct((4, 4, HALF, D + 128), bf16),
        ],
        compiler_params=pltpu.CompilerParams(vmem_limit_bytes=56 * 2**20),
        cost_estimate=pl.CostEstimate(
            flops=14 * 10**9, bytes_accessed=30 * 2**20, transcendentals=10**6
        ),
        name="experts",
    )(e, rows_a, rows_b, cot_all, router, w)


def weight_kernel(inputs, dres, dboth, hidden, out):
    for j in range(2):
        out[:, :, j * 1024 : (j + 1) * 1024] = (
            dot(inputs[j], dboth[j], TN).astype(bf16).reshape(2, LP, 1024)
        )
        out[:, :, 2048 + j * FF : 2048 + (j + 1) * FF] = (
            dot(dres[j], hidden[j], TN).astype(bf16).reshape(2, LP, FF)
        )


def expert_weights(inputs, dres, dboth, hidden):
    rows = NE * SLOTS
    return pl.pallas_call(
        weight_kernel,
        grid=(4,),
        in_specs=[
            pl.BlockSpec((2, rows, 256), lambda i: (0, 0, i)),
            pl.BlockSpec((2, rows, 256), lambda i: (0, 0, i)),
            pl.BlockSpec((2, rows, 2 * FF), lambda i: (0, 0, 0)),
            pl.BlockSpec((2, rows, FF), lambda i: (0, 0, 0)),
        ],
        out_specs=pl.BlockSpec((2, LP, 3072), lambda i: (i, 0, 0)),
        out_shape=jax.ShapeDtypeStruct((NF, LP, 3072), bf16),
        compiler_params=pltpu.CompilerParams(vmem_limit_bytes=26 * 2**20),
        cost_estimate=pl.CostEstimate(
            flops=7 * 10**9, bytes_accessed=20 * 2**20, transcendentals=0
        ),
        name="expert_weights",
    )(inputs, dres, dboth, hidden)


def swap_fsdp(v):
    return lax.all_to_all(v, "fsdp", split_axis=0, concat_axis=0, tiled=True)


def rope_tables():
    exponent = np.arange(HEAD_DIM // 2, dtype=np.float32) * np.float32(2.0 / HEAD_DIM)
    inverse = np.power(np.float32(rope_base), -exponent).astype(np.float32)
    angles = np.arange(LENGTH, dtype=np.float32)[:, None] * inverse[None, :]
    wide = np.tile(angles.astype(np.float32), (1, 4))
    return np.cos(wide).astype(np.float32), np.sin(wide).astype(np.float32)


def masked_gates(logits, member):
    low = jnp.where(member, logits, -1e30)
    top = jnp.max(low, axis=-1, keepdims=True)
    expo = jnp.where(member, jnp.exp(low - top), 0.0)
    return expo / jnp.sum(expo, axis=-1, keepdims=True)


def norm_back(u, v, gain):
    r = lax.rsqrt(jnp.mean(v * v, axis=-1, keepdims=True) + epsilon)
    inner = jnp.mean(gain * u * v, axis=-1, keepdims=True)
    return r * gain * u - v * (r * r * r) * inner, jnp.sum(u * v * r, axis=0)


def masked_scores(q_h, keys, seg_col, seg_row, first):
    rows, count = q_h.shape[0], keys.shape[0]
    scores = dot(q_h, keys, NT) * HEAD_DIM**-0.5
    row = lax.broadcasted_iota(jnp.int32, (rows, count), 0) + first
    column = lax.broadcasted_iota(jnp.int32, (rows, count), 1)
    allowed = (seg_col == seg_row) & (column <= row)
    return jnp.where(allowed, scores, -1e30)


QB = 256


def order_rows(core, mine, other, out):
    for x in range(4):
        own = pl.multiple_of(x * 2 * LP + core * LP, LP)
        out[pl.ds(own, LP)] = mine[x]
        beside = pl.multiple_of(x * 2 * LP + (1 - core) * LP, LP)
        out[pl.ds(beside, LP)] = other[x]


def pack_kernel(w_query, w_key, w_value, w_router, gains, out):
    rest = jnp.concatenate(
        [w_router[...], gains[...], jnp.zeros((LP, 128 - EXPERTS - 2), bf16)], axis=1
    )
    for f in range(NF):
        out[f, :, :128] = w_query[:, f * 128 : (f + 1) * 128]
        out[f, :, 128:192] = w_key[:, f * 64 : (f + 1) * 64]
        out[f, :, 192:256] = w_value[:, f * 64 : (f + 1) * 64]
        out[f, :, 256:] = rest


def pack(*operands):
    return pl.pallas_call(
        pack_kernel,
        out_shape=jax.ShapeDtypeStruct((NF, LP, 384), bf16),
        cost_estimate=pl.CostEstimate(flops=10**6, bytes_accessed=2 * 2**20, transcendentals=0),
        name="pack",
    )(*operands)


def half_swap(v):
    lane = lax.broadcasted_iota(jnp.int32, v.shape, 1)
    return jnp.where(lane % 64 < 32, -pltpu.roll(v, 96, 1), pltpu.roll(v, 32, 1))


def attend_kernel(
    core,
    mine,
    other,
    got,
    cos,
    sin,
    seg_col,
    seg_row,
    x,
    normed,
    qkv,
    attended,
    attended_send,
    lse,
    rest,
):
    order_rows(core[0], mine, other, x)
    for f in range(NF):
        part = slice(f * LP, (f + 1) * LP)
        rest[:, part] = jnp.transpose(got[part, 256:].astype(f32))[: EXPERTS + 8]
    x_full = x[...].astype(f32)
    r = lax.rsqrt(jnp.mean(x_full * x_full, axis=-1, keepdims=True) + epsilon)
    normed[...] = (x_full * r * rest[EXPERTS : EXPERTS + 1]).astype(bf16)
    raw = dot(normed[...], got[:, :256])
    turned = lax.broadcasted_iota(jnp.int32, (1, 128), 1) < HEAD_DIM
    cos_k, sin_k = jnp.where(turned, cos[...], 1.0), jnp.where(turned, sin[...], 0.0)
    raw_q, raw_kv = raw[:, :128], raw[:, 128:]
    qkv[:, :128] = (raw_q * cos[...] + half_swap(raw_q) * sin[...]).astype(bf16)
    qkv[:, 128:] = (raw_kv * cos_k + half_swap(raw_kv) * sin_k).astype(bf16)
    for i in range(LENGTH // QB):
        part, count = slice(i * QB, (i + 1) * QB), (i + 1) * QB
        keys, values = qkv[:count, 128:192], qkv[:count, 192:256]
        for h in range(2):
            scores = masked_scores(
                qkv[part, h * 64 : (h + 1) * 64], keys, seg_col[part], seg_row[:, :count], i * QB
            )
            top = jnp.max(scores, axis=-1, keepdims=True)
            expo = jnp.exp(scores - top)
            total = jnp.sum(expo, axis=-1, keepdims=True)
            probs = (expo * (1.0 / total)).astype(bf16)
            attended[part, h * 64 : (h + 1) * 64] = dot(probs, values).astype(bf16)
            lse[part, h : h + 1] = top + jnp.log(total)
        attended_send[2 * i : 2 * i + 2] = attended[part].reshape(2, LP, 128)


VMEM = pl.BlockSpec(memory_space=pltpu.VMEM)
SMEM = pl.BlockSpec(memory_space=pltpu.SMEM)


def attend(*operands):
    return pl.pallas_call(
        attend_kernel,
        in_specs=[SMEM] + [VMEM] * (len(operands) - 1),
        out_shape=[
            jax.ShapeDtypeStruct((LENGTH, D), bf16),
            jax.ShapeDtypeStruct((LENGTH, D), bf16),
            jax.ShapeDtypeStruct((LENGTH, 256), bf16),
            jax.ShapeDtypeStruct((LENGTH, 128), bf16),
            jax.ShapeDtypeStruct((NF, LP, 128), bf16),
            jax.ShapeDtypeStruct((LENGTH, 2), f32),
            jax.ShapeDtypeStruct((EXPERTS + 8, D), f32),
        ],
        compiler_params=pltpu.CompilerParams(vmem_limit_bytes=56 * 2**20),
        cost_estimate=pl.CostEstimate(
            flops=3 * 10**9, bytes_accessed=6 * 2**20, transcendentals=2 * 10**6
        ),
        name="attend",
    )(*operands)


def branch_back_kernel(core, mine, other, w_out, attended, part_output, dout, dbranch):
    order_rows(core[0], mine, other, dbranch)
    part_output[...] = dot(attended[...], dbranch[...], TN).astype(bf16)
    dout[...] = dot(dbranch[...], w_out[...], NT).astype(bf16)


def branch_back(*operands):
    return pl.pallas_call(
        branch_back_kernel,
        in_specs=[SMEM] + [VMEM] * (len(operands) - 1),
        out_shape=[
            jax.ShapeDtypeStruct((LP, D), bf16),
            jax.ShapeDtypeStruct((LENGTH, 128), bf16),
        ],
        scratch_shapes=[pltpu.VMEM((LENGTH, D), bf16)],
        compiler_params=pltpu.CompilerParams(vmem_limit_bytes=14 * 2**20),
        cost_estimate=pl.CostEstimate(
            flops=6 * 10**8, bytes_accessed=5 * 2**20, transcendentals=0
        ),
        name="branch_back",
    )(*operands)


def attend_back_kernel(
    x, normed, got, qkv, lse, dout, extra, cos, sin, seg_col, seg_row, payload, dnormed, dq, dkv
):
    dkv[...] = jnp.zeros_like(dkv)
    scale = HEAD_DIM**-0.5
    for i in range(LENGTH // QB):
        part, count = slice(i * QB, (i + 1) * QB), (i + 1) * QB
        keys, values = qkv[:count, 128:192], qkv[:count, 192:256]
        dk_part, dv_part = 0.0, 0.0
        for h in range(2):
            q_h, do_h = qkv[part, h * 64 : (h + 1) * 64], dout[part, h * 64 : (h + 1) * 64]
            scores = masked_scores(q_h, keys, seg_col[part], seg_row[:, :count], i * QB)
            probs = jnp.exp(scores - lse[part, h : h + 1])
            dprobs = dot(do_h, values, NT)
            delta = jnp.sum(probs * dprobs, axis=-1, keepdims=True)
            dscores = (probs * (dprobs - delta)).astype(bf16)
            dq[part, h * 64 : (h + 1) * 64] = dot(dscores, keys) * scale
            dk_part = dk_part + dot(dscores, q_h, TN)
            dv_part = dv_part + dot(probs.astype(bf16), do_h, TN)
        dkv[:count, :64] += dk_part * scale
        dkv[:count, 64:] += dv_part
    d_q, d_kv = dq[...], dkv[...]
    turned = lax.broadcasted_iota(jnp.int32, (1, 128), 1) < HEAD_DIM
    cos_k, sin_k = jnp.where(turned, cos[...], 1.0), jnp.where(turned, sin[...], 0.0)
    d_q = (d_q * cos[...] - half_swap(d_q) * sin[...]).astype(bf16)
    d_kv = (d_kv * cos_k - half_swap(d_kv) * sin_k).astype(bf16)
    dqkv = jnp.concatenate([d_q, d_kv], axis=1)
    payload[:, :256] = dot(normed[...], dqkv, TN).astype(bf16)
    d_n = dot(dqkv, got[:, :256], NT)
    dnormed[...] = d_n.astype(bf16).reshape(NF, LP, D)
    x_full = x[...].astype(f32)
    r = lax.rsqrt(jnp.mean(x_full * x_full, axis=-1, keepdims=True) + epsilon)
    dgain = jnp.sum(d_n * (x_full * r), axis=0, keepdims=True)
    lane = lax.broadcasted_iota(jnp.int32, (LP, 128), 1)
    for f in range(NF):
        part = slice(f * LP, (f + 1) * LP)
        column = jnp.transpose(jnp.broadcast_to(dgain[:, part], (128, LP)))
        payload[part, 256:] = jnp.where(
            lane == EXPERTS + 1, column, extra[part].astype(f32)
        ).astype(bf16)


def attend_back(*operands):
    return pl.pallas_call(
        attend_back_kernel,
        out_shape=[
            jax.ShapeDtypeStruct((LENGTH, 384), bf16),
            jax.ShapeDtypeStruct((NF, LP, D), bf16),
        ],
        scratch_shapes=[
            pltpu.VMEM((LENGTH, 128), f32),
            pltpu.VMEM((LENGTH, 128), f32),
        ],
        compiler_params=pltpu.CompilerParams(vmem_limit_bytes=56 * 2**20),
        cost_estimate=pl.CostEstimate(
            flops=6 * 10**9, bytes_accessed=14 * 2**20, transcendentals=2 * 10**6
        ),
        name="attend_back",
    )(*operands)


def unpack_kernel(
    total, grads, query, key, value, output, router_t, gain_two, gain_one, gate, up, down
):
    query[...] = total[:, :1024].astype(f32)
    key[...] = total[:, 1024:1536].astype(f32)
    value[...] = total[:, 1536:2048].astype(f32)
    output[...] = total[:, 2176:].astype(f32)
    rest_t = jnp.transpose(total[:, 2048:2176].astype(f32))
    router_t[...] = rest_t[:EXPERTS]
    gain_two[...] = rest_t[EXPERTS : EXPERTS + 1]
    gain_one[...] = rest_t[EXPERTS + 1 : EXPERTS + 2]
    for j in range(2):
        gate[j] = grads[:, j * 1024 : j * 1024 + FF].astype(f32)
        up[j] = grads[:, j * 1024 + FF : (j + 1) * 1024].astype(f32)
        down[j] = jnp.transpose(grads[:, 2048 + j * FF : 2048 + (j + 1) * FF].astype(f32))


def unpack(total, grads):
    shapes = [(LP, D), (LP, FF), (LP, FF), (LP, D), (EXPERTS, LP), (1, LP), (1, LP)]
    shapes += [(2, LP, FF), (2, LP, FF), (2, FF, LP)]
    return pl.pallas_call(
        unpack_kernel,
        out_shape=[jax.ShapeDtypeStruct(shape, f32) for shape in shapes],
        cost_estimate=pl.CostEstimate(flops=10**6, bytes_accessed=6 * 2**20, transcendentals=0),
        name="unpack",
    )(total, grads)


HEAD_PARTS = (slice(0, 128), slice(128, 192), slice(192, 256))


def local(
    layer_input,
    segment_ids,
    routes,
    attn_gain,
    w_query,
    w_key,
    w_value,
    w_output,
    w_router,
    ffn_gain,
    w_gate,
    w_up,
    w_down,
    cotangent,
):
    e = lax.axis_index("expert")
    x_own = layer_input[0]
    cot_own = cotangent[0]
    payload = pack(
        w_query, w_key, w_value, w_router, jnp.stack([attn_gain, ffn_gain], axis=1)
    )
    core = (lax.axis_index("fsdp") % 2)[None]
    x_mine, x_other, got = gather_fsdp(x_own, swap_fsdp(payload))
    got = got.reshape(D, 384)
    cot_all = lax.all_gather(
        jnp.concatenate(
            [
                cot_own,
                jnp.pad(routes[0].astype(bf16).T, ((0, 8), (0, D - LP))),
            ],
            axis=0,
        ),
        "expert",
        axis=0,
    )

    cos_wide, sin_wide = (jnp.asarray(table) for table in rope_tables())
    seg_row = segment_ids
    seg_col = segment_ids.reshape(LENGTH, 1)
    x_all, normed, qkv, attended, attended_send, lse, rest = attend(
        core, x_mine, x_other, got, cos_wide, sin_wide, seg_col, seg_row
    )
    router_t = rest[:EXPERTS].astype(bf16)
    gain_one, gain_two = rest[EXPERTS], rest[EXPERTS + 1]
    w_mine, w_other, attended_send = gather_fsdp(after(w_output, x_other), attended_send)
    w_out = in_order(w_mine, w_other)
    member_own = jnp.any(
        routes[0][:, :, None] == jnp.arange(EXPERTS, dtype=jnp.int32), axis=1
    )

    attended_own = swap_fsdp(attended_send).swapaxes(0, 1).reshape(LP, D)
    w_own = jnp.concatenate(
        [w_gate[0], w_up[0], w_gate[1], w_up[1], w_down[0].T, w_down[1].T], axis=1
    )
    w_own = after(w_own, attended_own)
    w_exp = lax.all_gather(w_own, "fsdp", axis=0, tiled=True)
    after_attn = x_own.astype(f32) + jnp.dot(attended_own, w_out, preferred_element_type=f32)
    r_two = lax.rsqrt(jnp.mean(after_attn * after_attn, axis=-1, keepdims=True) + epsilon)
    normed_two = (after_attn * r_two * gain_two).astype(bf16)

    rows_a, rows_b = gather_expert(normed_two)
    inputs, hidden, dboth, dres, mix_part, drows_a, drows_b = experts(
        e[None], rows_a, rows_b, cot_all, router_t, w_exp
    )
    mix = lax.psum_scatter(mix_part, "expert", scatter_dimension=0)
    grad_exp = expert_weights(inputs, dres, dboth, hidden)
    drows, grad_exp = scatter_expert(drows_a, drows_b, grad_exp)
    grad_exp = lax.psum_scatter(grad_exp, "fsdp", scatter_dimension=0)

    logits = jnp.einsum("td,ed->te", normed_two, router_t, preferred_element_type=f32)
    gates = masked_gates(logits, member_own)
    dgate_own = drows[:, D : D + EXPERTS] + drows[:, D + EXPERTS : D + 2 * EXPERTS]
    dlogits = gates * (dgate_own - jnp.sum(gates * dgate_own, axis=-1, keepdims=True))
    dnormed_two = drows[:, :D] + jnp.einsum(
        "te,ed->td", dlogits, router_t.astype(f32), precision=highest
    )
    dafter_norm, part_gain_two = norm_back(dnormed_two, after_attn, gain_two)
    dafter = cot_own.astype(f32) + dafter_norm
    dbranch = dafter.astype(bf16)
    d_mine, d_other, _ = gather_fsdp(dbranch)
    part_router = jnp.einsum(
        "td,te->de", normed_two.astype(f32), dlogits, precision=highest
    )

    extra = jnp.concatenate(
        [
            part_router.astype(bf16),
            part_gain_two[:, None].astype(bf16),
            jnp.zeros((D, 128 - EXPERTS - 1), bf16),
        ],
        axis=-1,
    )

    part_output, dout = branch_back(core, d_mine, d_other, w_output, attended)
    part_output = lax.all_to_all(
        part_output.reshape(NE, LP // NE, D), "expert", split_axis=0, concat_axis=0, tiled=True
    )
    payload, dnormed_part = attend_back(
        x_all, normed, got, qkv, lse, dout, extra, cos_wide, sin_wide, seg_col, seg_row
    )
    payload, dnormed_part, mix, part_output = lax.optimization_barrier(
        (payload, dnormed_part, mix, part_output)
    )
    layer_output = (after_attn + mix.astype(f32)).astype(bf16)
    dnormed_pair = pair_sum(dnormed_part)
    small = lax.all_to_all(
        payload.reshape(NF * NE, LP // NE, 384),
        ("fsdp", "expert"),
        split_axis=0,
        concat_axis=0,
        tiled=True,
    )
    small = jnp.sum(small.reshape(NF, NE, LP // NE, 384).astype(f32), axis=1)
    chunk_output = jnp.sum(part_output.astype(f32), axis=0)
    chunk = jnp.concatenate(
        [small[:, :, part].swapaxes(0, 1).reshape(LP // NE, -1) for part in HEAD_PARTS]
        + [jnp.sum(small[:, :, 256:], axis=0), chunk_output],
        axis=-1,
    ).astype(bf16)
    chunk, dnormed_pair = lax.optimization_barrier((chunk, dnormed_pair))
    total_sum = lax.all_to_all(
        jnp.broadcast_to(chunk[None], (NE,) + chunk.shape),
        "expert",
        split_axis=0,
        concat_axis=0,
        tiled=True,
    ).reshape(LP, 3200)
    dnormed = ring_sum(shift_x, dnormed_pair, lax.axis_index("fsdp") // 2)
    dinput_norm, _ = norm_back(dnormed, x_own.astype(f32), gain_one)
    grad_input = (dafter + dinput_norm).astype(bf16)
    (
        grad_query,
        grad_key,
        grad_value,
        grad_output,
        grad_router_t,
        grad_gain_two,
        grad_gain_one,
        grad_gate,
        grad_up,
        grad_down,
    ) = unpack(total_sum, grad_exp)
    return (
        layer_output[None],
        grad_input[None],
        grad_gain_one.reshape(LP),
        grad_query,
        grad_key,
        grad_value,
        grad_output,
        grad_router_t.T,
        grad_gain_two.reshape(LP),
        grad_gate,
        grad_up,
        grad_down,
    )


def solution(mesh):
    placed = (
        P("expert", "fsdp", None),
        P("expert", None),
        P("expert", "fsdp", None),
        P("fsdp"),
        P("fsdp", None),
        P("fsdp", None),
        P("fsdp", None),
        P("fsdp", None),
        P("fsdp", None),
        P("fsdp"),
        P("expert", "fsdp", None),
        P("expert", "fsdp", None),
        P("expert", None, "fsdp"),
        P("expert", "fsdp", None),
    )
    return jax.shard_map(
        local,
        mesh=mesh,
        in_specs=placed,
        out_specs=(
            P("expert", "fsdp", None),
            P("expert", "fsdp", None),
            P("fsdp"),
            P("fsdp", None),
            P("fsdp", None),
            P("fsdp", None),
            P("fsdp", None),
            P("fsdp", None),
            P("fsdp"),
            P("expert", "fsdp", None),
            P("expert", "fsdp", None),
            P("expert", None, "fsdp"),
        ),
        check_vma=False,
    )
```
